256 devices in a mesh: chan: 128 (over y, z, x_lo, core), tm: 2 (over x_hi).
Axes of the slice: x: 4 (x_hi: 2, x_lo: 2; x = x_hi * 2 + x_lo), y: 4, z: 8, core: 2. Of those that a mesh axis runs over, the one named last changes fastest.
Arguments:
- traces: float32 [4, 1024, 768], P('tm', 'chan'), may hold values from -6 to 6
- lengths: int32 [4], replicated, may hold values from 1 to 768, 2304 in all
- mask: int32 [1024], P('chan'), may hold values 0 or 1
Outputs:
- correlations: float32 [1024, 1024, 256], P(('chan', 'tm'))
The draws below stay inside these ranges and needn't reach their ends.
Inputs may be any that keep to these rules, and one draw needn't show every extreme that they name: `lengths`: live samples of each sub-window; together they hold 2304 samples and the longest holds exactly 768.
All inputs are finite; a program needn't handle non-finite values. No bound on the sum of `mask` on one device may be relied on, other than what follows from the above.
Results may differ from the reference program's by a relative error of at most 0.0043.
Values may be sent and summed in bfloat16 or wider, within the bound.
No kernel may reach another device: no remote copies, remote signals or barrier semaphores. Data moves between devices by JAX's collectives and lax.ppermute only.
A program may use at most 128 MiB of HBM per device.

```python
import math
import jax
import jax.numpy as jnp
import numpy as np
from jax import lax

CH_DEV = 8
NFFT = 1024
SEG = 768
LAG = 128
F = 512
CHANNELS = 1024
SUBWIN = 4
N_TM = 2


def set_ends(array, stream_key, smallest, top_value):
    place = [jax.random.randint(jax.random.fold_in(stream_key, axis), (), 0, length) for axis, length in enumerate(array.shape)]
    main_axis = array.shape.index(max(array.shape))
    neighbour = place[:main_axis] + [(place[main_axis] + 1) % array.shape[main_axis]] + place[main_axis + 1:]
    return array.at[tuple(place)].set(smallest).at[tuple(neighbour)].set(top_value)


def level_of(rng, extent, cuts, smallest, high):
    gain, own = 1.0, jax.random.fold_in(rng, 6)
    for axis_at, blocks in cuts:
        heights = jnp.exp(jax.random.uniform(jax.random.fold_in(own, axis_at), (blocks,), jnp.float32, smallest / len(cuts), high / len(cuts)))
        gain = gain * jnp.repeat(heights, extent[axis_at] // blocks).reshape([-1 if axis == axis_at else 1 for axis in range(len(extent))])
    return gain


def split_up(number_of, total, limit, skew):
    portions = [(1 << 20) // math.isqrt(grade ** skew) + 1 for grade in range(2, number_of + 1)]
    surplus, given = total - limit - (number_of - 1), [1] * (number_of - 1)
    while surplus > 0:
        free = [i for i in range(number_of - 1) if given[i] < limit]
        pool, remaining = sum([portions[i] for i in free]), surplus
        for i in free:
            more = min(limit - given[i], max(1, remaining * portions[i] // pool), surplus)
            given[i] = given[i] + more
            surplus = surplus - more
    return np.array([limit] + given)


def uneven_parts(own_key, number_of, total, reach, skew):
    if number_of == 2:
        one = jax.random.randint(own_key, (), max(1, total - reach), min(reach, total - 1) + 1)
        return jnp.stack([one, total - one])
    sizes = jnp.asarray(split_up(number_of, total, reach, skew), jnp.int32)
    twos = (number_of - 1) // 2
    donor, sink = sizes[1:1 + 2 * twos:2], sizes[2:2 + 2 * twos:2]
    slack = jnp.minimum(donor - 1, reach - sink)
    shifted = jax.random.randint(jax.random.fold_in(own_key, 1), (twos,), 0, 1 << 20) % (slack + 1)
    sizes = sizes.at[1:1 + 2 * twos:2].set(donor - shifted).at[2:2 + 2 * twos:2].set(sink + shifted)
    return sizes[jax.random.permutation(jax.random.fold_in(own_key, 2), number_of)]


def noise(stream_key, dims, width, reach, split=(), held_as=jnp.bfloat16):
    drawn = width * jax.random.normal(stream_key, dims, jnp.float32)
    if split:
        drawn = drawn * level_of(stream_key, dims, split, -0.22, 0.18)
    return jnp.clip(drawn, -reach, reach).astype(held_as)


def setup_inputs(seed: int = 0) -> dict:
    streams_of = jax.random.split(jax.random.key(seed), 4)
    return {
        "traces": noise(streams_of[0], (SUBWIN, CHANNELS, SEG), 1.0, 6.0, ((0, 2), (1, 128)), jnp.float32),
        "lengths": uneven_parts(streams_of[1], SUBWIN, SUBWIN * SEG * 3 // 4, SEG, 2).astype(jnp.int32),
        "mask": set_ends((jax.random.randint(streams_of[2], (CHANNELS,), 0, 8) < 7).astype(jnp.int32), jax.random.fold_in(streams_of[2], 1), 0, 1),
    }


def dft_table(seg_len, nfft, nfreq):
    sample_idx = jnp.arange(seg_len, dtype=jnp.int32)
    freq_idx = jnp.arange(nfreq, dtype=jnp.int32)
    product = jnp.mod(sample_idx[:, None] * freq_idx[None, :], nfft).astype(jnp.float32)
    theta = product * (2.0 * math.pi / nfft)
    return jnp.concatenate([jnp.cos(theta), -jnp.sin(theta)], axis=1)

def lag_table(nfft, nfreq, max_lag, sub_total):
    freq_idx = jnp.arange(nfreq, dtype=jnp.int32)
    lag_idx = jnp.arange(2 * max_lag, dtype=jnp.int32) - max_lag
    product = jnp.mod(freq_idx[:, None] * lag_idx[None, :], nfft).astype(jnp.float32)
    phase = product * (2.0 * math.pi / nfft)
    weight = jnp.where(freq_idx == 0, 1.0, 2.0).astype(jnp.float32)[:, None] / math.sqrt(nfreq * sub_total)
    return jnp.concatenate([weight * jnp.cos(phase), -weight * jnp.sin(phase)], axis=0).astype(jnp.bfloat16)

def whiten_spectra(traces, lengths, mask):
    seg_len = traces.shape[2]
    live = (jnp.arange(seg_len, dtype=jnp.int32)[None, :] < lengths[:, None]).astype(jnp.float32)
    counted = lengths.astype(jnp.float32)
    average = lax.optimization_barrier(jnp.sum(traces * live[:, None, :], axis=-1)) / counted[:, None]
    centred = (traces - average[:, :, None]) * live[:, None, :]
    table = dft_table(seg_len, NFFT, F)
    spectrum = jnp.dot(centred.reshape(-1, seg_len), table, precision=lax.Precision.HIGHEST, preferred_element_type=jnp.float32)
    spectrum = spectrum.reshape(traces.shape[0], traces.shape[1], 2 * F)
    power = spectrum[..., :F] ** 2 + spectrum[..., F:] ** 2
    level = lax.optimization_barrier(jnp.mean(power, axis=-1, keepdims=True))
    factor = 1.0 / jnp.sqrt(power + 0.01 * level + 1e-06)
    factor = jnp.concatenate([factor, factor], axis=-1)
    return (spectrum * factor * mask.astype(jnp.float32)[None, :, None]).astype(jnp.bfloat16)

def cross_spectrum(own_spec, other_spec):
    nfreq = own_spec.shape[-1] // 2
    own_re = own_spec[..., :nfreq].astype(jnp.float32)
    own_im = own_spec[..., nfreq:].astype(jnp.float32)
    other_re = other_spec[..., :nfreq].astype(jnp.float32)
    other_im = other_spec[..., nfreq:].astype(jnp.float32)
    real_part = jnp.einsum('kif,kjf->ijf', own_re, other_re) + jnp.einsum('kif,kjf->ijf', own_im, other_im)
    imag_part = jnp.einsum('kif,kjf->ijf', own_im, other_re) - jnp.einsum('kif,kjf->ijf', own_re, other_im)
    return jnp.concatenate([real_part, imag_part], axis=-1).astype(jnp.bfloat16)

def reference(traces, lengths, mask):
    spectra = whiten_spectra(traces, lengths, mask)
    lag_matrix = lag_table(NFFT, F, LAG, SUBWIN)
    stacked = jnp.concatenate([lag_matrix] * N_TM, axis=0)
    sub_count = SUBWIN // N_TM

    def one_block(block_index):
        own_spec = lax.dynamic_slice_in_dim(spectra, block_index * CH_DEV, CH_DEV, axis=1)
        half_spectra = [cross_spectrum(own_spec[h * sub_count:(h + 1) * sub_count], spectra[h * sub_count:(h + 1) * sub_count]) for h in range(N_TM)]
        joined = jnp.concatenate(half_spectra, axis=-1)
        lag_values = jnp.dot(joined.reshape(CH_DEV * CHANNELS, joined.shape[-1]), stacked, preferred_element_type=jnp.float32)
        return lag_values.reshape(CH_DEV, CHANNELS, 2 * LAG)
    blocks = lax.map(one_block, jnp.arange(CHANNELS // CH_DEV, dtype=jnp.int32))
    return blocks.reshape(CHANNELS, CHANNELS, 2 * LAG)
```

```python
import math

import jax
import jax.numpy as jnp
import ml_dtypes
import numpy as np
from jax import lax
from jax.experimental import pallas as pl
from jax.experimental.pallas import tpu as pltpu
from jax.sharding import Mesh
from jax.sharding import PartitionSpec as P

NFFT = 1024
LAG = 128
F = 512
SEG = 768
SUBWIN = 4
NY, NZ, NX = 4, 8, 4
AXES = ("y", "z", "xl", "core", "tm")
VMEM_LIMIT = 60 * 2**20


def dft_tables():
    product = np.mod(np.arange(SEG)[:, None] * np.arange(F)[None, :], NFFT)
    theta = product * (2.0 * math.pi / NFFT)
    table = np.concatenate([np.cos(theta), -np.sin(theta)], axis=1)
    high = table.astype(ml_dtypes.bfloat16)
    low = (table - high.astype(np.float64)).astype(ml_dtypes.bfloat16)
    return high, low


def lag_table():
    product = np.mod(np.arange(F)[:, None] * (np.arange(2 * LAG) - LAG)[None, :], NFFT)
    phase = product * (2.0 * math.pi / NFFT)
    weight = np.where(np.arange(F) == 0, 1.0, 2.0)[:, None] / math.sqrt(F * SUBWIN)
    table = np.concatenate([weight * np.cos(phase), -weight * np.sin(phase)], axis=0)
    return table.astype(np.float32).astype(ml_dtypes.bfloat16)


def device_index(y, z, x, core):
    return (((y * NZ + z) * 2 + x % 2) * 2 + core) * 2 + x // 2


def permute(value, partner):
    pairs = []
    for y in range(NY):
        for z in range(NZ):
            for x in range(NX):
                for core in range(2):
                    pairs.append((device_index(y, z, x, core), device_index(*partner(y, z, x, core))))
    return lax.ppermute(value, AXES, pairs)


def along_z(d):
    return lambda y, z, x, core: (y, z ^ d, x, core)


def along_first(d):
    return lambda y, z, x, core: (y ^ d, z, x, core) if core == 0 else (y, z, x ^ d, core)


def along_second(d):
    return lambda y, z, x, core: (y, z, x ^ d, core) if core == 0 else (y ^ d, z, x, core)


def other_core(y, z, x, core):
    return (y, z, x, 1 - core)


def other_group(y, z, x, core):
    return (y, z, x ^ 2, core)


def whiten_kernel(lengths_ref, mask_ref, traces_ref, high_ref, low_ref, out_ref):
    tm = lax.axis_index("tm")
    x = traces_ref[...].reshape(16, SEG)
    row = lax.broadcasted_iota(jnp.int32, (16, 1), 0)
    length = jnp.where(row < 8, lengths_ref[2 * tm], lengths_ref[2 * tm + 1])
    usable = jnp.zeros((16, 1), jnp.float32)
    for c in range(8):
        usable = jnp.where(row % 8 == c, mask_ref[c].astype(jnp.float32), usable)
    live = lax.broadcasted_iota(jnp.int32, (16, SEG), 1) < length
    average = jnp.sum(jnp.where(live, x, 0.0), axis=1, keepdims=True) / length.astype(jnp.float32)
    centred = jnp.where(live, x - average, 0.0)
    part0 = centred.astype(jnp.bfloat16)
    rest = centred - part0.astype(jnp.float32)
    part1 = rest.astype(jnp.bfloat16)
    part2 = (rest - part1.astype(jnp.float32)).astype(jnp.bfloat16)
    parts = jnp.concatenate([part0, part1, part2], axis=0)
    by_high = jnp.dot(parts, high_ref[...], preferred_element_type=jnp.float32)
    by_low = jnp.dot(parts[:32], low_ref[...], preferred_element_type=jnp.float32)
    spectrum = by_high[:16] + (by_high[16:32] + by_low[:16] + (by_high[32:] + by_low[16:]))
    re, im = spectrum[:, :F], spectrum[:, F:]
    power = re * re + im * im
    level = jnp.mean(power, axis=1, keepdims=True)
    factor = usable / jnp.sqrt(power + 0.01 * level + 1e-06)
    for k in range(2):
        rows = slice(8 * k, 8 * k + 8)
        out_ref[:, 2 * k * F : (2 * k + 1) * F] = (re * factor)[rows].astype(jnp.bfloat16)
        out_ref[:, (2 * k + 1) * F : (2 * k + 2) * F] = (im * factor)[rows].astype(jnp.bfloat16)


def whiten(traces, lengths, mask):
    high, low = dft_tables()
    smem = pl.BlockSpec(memory_space=pltpu.SMEM)
    vmem = pl.BlockSpec(memory_space=pltpu.VMEM)
    return pl.pallas_call(
        whiten_kernel,
        in_specs=[smem, smem, vmem, vmem, vmem],
        out_specs=vmem,
        out_shape=jax.ShapeDtypeStruct((8, 4 * F), jnp.bfloat16),
        compiler_params=pltpu.CompilerParams(vmem_limit_bytes=VMEM_LIMIT),
        name="whiten",
    )(lengths, mask, traces, jnp.asarray(high), jnp.asarray(low))


def fold_kernel(own_ref, other_ref, lag_ref, out_ref, columns):
    tm = lax.axis_index("tm")
    own = own_ref[...].astype(jnp.float32)
    other = other_ref[...].astype(jnp.float32)
    rows = jnp.concatenate([own, other], axis=0)
    rows = jnp.where(tm == 0, jnp.concatenate([rows[0:4], rows[8:12]], axis=0), jnp.concatenate([rows[4:8], rows[12:16]], axis=0))
    columns[...] = rows.T
    step = 64

    @pl.loop(0, F, step=step)
    def _(begin):
        re_at = pl.ds(pl.multiple_of(begin, step), step)
        im_at = pl.ds(pl.multiple_of(begin + F, step), step)
        cos = lag_ref[re_at, :].astype(jnp.float32)
        sin = lag_ref[im_at, :].astype(jnp.float32)
        for group in range(2):
            for i in range(4):
                a_re = columns[re_at, 4 * group + i : 4 * group + i + 1]
                a_im = columns[im_at, 4 * group + i : 4 * group + i + 1]
                lanes = slice(2 * LAG * i, 2 * LAG * (i + 1))
                out_ref[group, 0, re_at, lanes] = (a_re * cos + a_im * sin).astype(jnp.bfloat16)
                out_ref[group, 0, im_at, lanes] = (a_im * cos - a_re * sin).astype(jnp.bfloat16)


def fold(own, other):
    folded = pl.pallas_call(
        fold_kernel,
        grid=(2,),
        in_specs=[
            pl.BlockSpec((8, 2 * F), lambda k: (0, k)),
            pl.BlockSpec((8, 2 * F), lambda k: (0, k)),
            pl.BlockSpec((2 * F, 2 * LAG), lambda k: (0, 0)),
        ],
        out_specs=pl.BlockSpec((2, 1, 2 * F, 8 * LAG), lambda k: (0, k, 0, 0)),
        out_shape=jax.ShapeDtypeStruct((2, 2, 2 * F, 8 * LAG), jnp.bfloat16),
        scratch_shapes=[pltpu.VMEM((2 * F, 8), jnp.float32)],
        compiler_params=pltpu.CompilerParams(vmem_limit_bytes=VMEM_LIMIT),
        name="fold",
    )(own, other, jnp.asarray(lag_table()))
    return folded.reshape(8 * F, 8 * LAG)


def correlate_kernel(*refs):
    mine, theirs, folded, out_ref = refs[0:4], refs[4:8], refs[8], refs[9]
    y, z, xl, core = (lax.axis_index(name) for name in ("y", "z", "xl", "core"))
    half = 4 * F

    def store(values, slot, e, kind):
        for g in range(NZ):
            out_ref[0, y ^ slot, z ^ g, xl ^ e, kind] = values[8 * g : 8 * g + 8]

    def product(first, second):
        return jnp.dot(first, folded[:half, :], preferred_element_type=jnp.float32) + jnp.dot(
            second, folded[half:, :], preferred_element_type=jnp.float32
        )

    def x_chunks(chunks):
        for e in range(2):
            values = product(chunks[e][...], chunks[e + 2][...])
            for slot in range(4):
                store(values[64 * slot : 64 * slot + 64], slot, e, 0)

    def y_chunks(chunks):
        for e in range(2):
            first = jnp.concatenate([chunks[b][64 * e : 64 * e + 64, :] for b in range(4)], axis=0)
            second = jnp.concatenate([chunks[b][64 * e + 128 : 64 * e + 192, :] for b in range(4)], axis=0)
            values = product(first, second)
            for slot in range(4):
                store(values[64 * slot : 64 * slot + 64], slot, e, 1)

    @pl.when(core == 0)
    def _():
        x_chunks(mine)
        y_chunks(theirs)

    @pl.when(core == 1)
    def _():
        y_chunks(mine)
        x_chunks(theirs)


def correlate(mine, theirs, folded):
    whole = pl.BlockSpec((256, 4 * F), lambda i: (0, 0))
    out = pl.pallas_call(
        correlate_kernel,
        grid=(4,),
        in_specs=[whole] * 8 + [pl.BlockSpec((8 * F, 2 * LAG), lambda i: (0, i))],
        out_specs=pl.BlockSpec((1, NY, NZ, 2, 2, 8, 2 * LAG), lambda i: (i, 0, 0, 0, 0, 0, 0)),
        out_shape=jax.ShapeDtypeStruct((4, NY, NZ, 2, 2, 8, 2 * LAG), jnp.float32),
        compiler_params=pltpu.CompilerParams(vmem_limit_bytes=VMEM_LIMIT),
        name="correlate",
    )(*mine, *theirs, folded)
    return out.reshape(4, NY * NZ * 4 * 8, 2 * LAG)


def local(traces, lengths, mask):
    own = whiten(traces, lengths, mask)
    other = permute(own, other_group)
    folded = fold(own, other)
    ring = jnp.concatenate([own] + [permute(own, along_z(d)) for d in range(1, 8)], axis=0)
    plane = jnp.concatenate([ring] + [permute(ring, along_first(d)) for d in range(1, 4)], axis=0)
    mine = [plane] + [permute(plane, along_second(d)) for d in range(1, 4)]
    theirs = [permute(chunk, other_core) for chunk in mine]
    return correlate(mine, theirs, folded)


def solution(mesh):
    finer = Mesh(mesh.devices.reshape(NY, NZ, 2, 2, 2), AXES)
    chan = ("y", "z", "xl", "core")
    return jax.shard_map(
        local,
        mesh=finer,
        in_specs=(P("tm", chan, None), P(), P(chan)),
        out_specs=P(AXES, None, None),
        check_vma=False,
    )
```

```python
import functools
import math

import jax
import jax.numpy as jnp
import ml_dtypes
import numpy as np
from jax import lax
from jax.experimental import pallas as pl
from jax.experimental.pallas import tpu as pltpu
from jax.sharding import Mesh
from jax.sharding import PartitionSpec as P

NFFT = 1024
LAG = 128
F = 512
SEG = 768
SUBWIN = 4
NY, NZ, NX = 4, 8, 4
AXES = ("y", "z", "xl", "core", "tm")


def dft_tables():
    product = np.mod(np.arange(SEG)[:, None] * np.arange(F)[None, :], NFFT)
    theta = product * (2.0 * math.pi / NFFT)
    table = np.concatenate([np.cos(theta), -np.sin(theta)], axis=1)
    high = table.astype(ml_dtypes.bfloat16)
    low = (table - high.astype(np.float64)).astype(ml_dtypes.bfloat16)
    return high, low


def lag_table():
    product = np.mod(np.arange(F)[:, None] * (np.arange(2 * LAG) - LAG)[None, :], NFFT)
    phase = product * (2.0 * math.pi / NFFT)
    weight = np.where(np.arange(F) == 0, 1.0, 2.0)[:, None] / math.sqrt(F * SUBWIN)
    table = np.concatenate([weight * np.cos(phase), -weight * np.sin(phase)], axis=0)
    return table.astype(np.float32).astype(ml_dtypes.bfloat16)


def device_index(y, z, x, core):
    return (((y * NZ + z) * 2 + x % 2) * 2 + core) * 2 + x // 2


def permute(value, partner):
    pairs = []
    for y in range(NY):
        for z in range(NZ):
            for x in range(NX):
                for core in range(2):
                    pairs.append((device_index(y, z, x, core), device_index(*partner(y, z, x, core))))
    return lax.ppermute(value, AXES, pairs)


def along_z(d):
    return lambda y, z, x, core: (y, z ^ d, x, core)


def along_first(d):
    return lambda y, z, x, core: (y ^ d, z, x, core) if core == 0 else (y, z, x ^ d, core)


def along_second(d):
    return lambda y, z, x, core: (y, z, x ^ d, core) if core == 0 else (y ^ d, z, x, core)


def other_core(y, z, x, core):
    return (y, z, x, 1 - core)


def other_group(y, z, x, core):
    return (y, z, x ^ 2, core)


def whiten_kernel(lengths_ref, mask_ref, traces_ref, high_ref, low_ref, out_ref):
    tm = lax.axis_index("tm")
    x = traces_ref[...].reshape(16, SEG)
    row = lax.broadcasted_iota(jnp.int32, (16, 1), 0)
    length = jnp.where(row < 8, lengths_ref[2 * tm], lengths_ref[2 * tm + 1])
    usable = jnp.zeros((16, 1), jnp.float32)
    for c in range(8):
        usable = jnp.where(row % 8 == c, mask_ref[c].astype(jnp.float32), usable)
    live = lax.broadcasted_iota(jnp.int32, (16, SEG), 1) < length
    average = jnp.sum(jnp.where(live, x, 0.0), axis=1, keepdims=True) / length.astype(jnp.float32)
    centred = jnp.where(live, x - average, 0.0)
    part0 = centred.astype(jnp.bfloat16)
    rest = centred - part0.astype(jnp.float32)
    part1 = rest.astype(jnp.bfloat16)
    part2 = (rest - part1.astype(jnp.float32)).astype(jnp.bfloat16)
    parts = jnp.concatenate([part0, part1, part2], axis=0)
    by_high = jnp.dot(parts, high_ref[...], preferred_element_type=jnp.float32)
    by_low = jnp.dot(parts[:32], low_ref[...], preferred_element_type=jnp.float32)
    spectrum = by_high[:16] + (by_high[16:32] + by_low[:16] + (by_high[32:] + by_low[16:]))
    re, im = spectrum[:, :F], spectrum[:, F:]
    power = re * re + im * im
    level = jnp.mean(power, axis=1, keepdims=True)
    factor = usable / jnp.sqrt(power + 0.01 * level + 1e-06)
    for k in range(2):
        rows = slice(8 * k, 8 * k + 8)
        out_ref[:, 2 * k * F : (2 * k + 1) * F] = (re * factor)[rows].astype(jnp.bfloat16)
        out_ref[:, (2 * k + 1) * F : (2 * k + 2) * F] = (im * factor)[rows].astype(jnp.bfloat16)


def whiten(traces, lengths, mask):
    high, low = dft_tables()
    smem = pl.BlockSpec(memory_space=pltpu.SMEM)
    vmem = pl.BlockSpec(memory_space=pltpu.VMEM)
    return pl.pallas_call(
        whiten_kernel,
        in_specs=[smem, smem, vmem, vmem, vmem],
        out_specs=vmem,
        out_shape=jax.ShapeDtypeStruct((8, 4 * F), jnp.bfloat16),
        compiler_params=pltpu.CompilerParams(vmem_limit_bytes=60 * 2**20),
        name="whiten",
    )(lengths, mask, traces, jnp.asarray(high), jnp.asarray(low))


def fold_kernel(own_ref, other_ref, lag_ref, out_ref, rows):
    i = pl.program_id(0)
    rows[0] = own_ref[...].astype(jnp.float32)
    rows[1] = other_ref[...].astype(jnp.float32)
    mine = 4 * lax.axis_index("tm") + i
    step = 32

    @pl.loop(0, 2 * LAG, step=step)
    def _(begin):
        at = pl.ds(pl.multiple_of(begin, step), step)
        cos = lag_ref[at, :F].astype(jnp.float32)
        sin = lag_ref[at, F:].astype(jnp.float32)
        for group in range(2):
            for k in range(2):
                to = 2 * F * (2 * group + k)
                a_re = rows[group, pl.ds(mine, 1), 2 * k * F : (2 * k + 1) * F]
                a_im = rows[group, pl.ds(mine, 1), (2 * k + 1) * F : (2 * k + 2) * F]
                out_ref[at, to : to + F] = (a_re * cos + a_im * sin).astype(jnp.bfloat16)
                out_ref[at, to + F : to + 2 * F] = (a_im * cos - a_re * sin).astype(jnp.bfloat16)


def fold(own, other):
    whole = pl.BlockSpec((8, 4 * F), lambda i: (0, 0))
    return pl.pallas_call(
        fold_kernel,
        grid=(4,),
        in_specs=[whole, whole, pl.BlockSpec((2 * LAG, 2 * F), lambda i: (0, 0))],
        out_specs=pl.BlockSpec((2 * LAG, 8 * F), lambda i: (i, 0)),
        out_shape=jax.ShapeDtypeStruct((8 * LAG, 8 * F), jnp.bfloat16),
        scratch_shapes=[pltpu.VMEM((2, 8, 4 * F), jnp.float32)],
        cost_estimate=pl.CostEstimate(flops=2**20, bytes_accessed=2**10, transcendentals=0),
        compiler_params=pltpu.CompilerParams(vmem_limit_bytes=16 * 2**20),
        name="fold",
    )(own, other, jnp.asarray(np.ascontiguousarray(lag_table().T)))


def select(part, x, y):
    if part == 0:
        return [y[0][:128, :]], [y[0][128:, :]]
    if part == 1:
        return [x[0][...], y[0][:128, :], y[1][:128, :]], [x[1][...], y[0][128:, :], y[1][128:, :]]
    return [x[0][...], y[1][...]], [x[1][...], x[2][...], y[2][...]]


def places_of(part, y, xl):
    if part == 0:
        return [(y, xl ^ e, 1) for e in range(2)]
    if part == 1:
        return [(y ^ b, xl ^ 1, 0) for b in range(4)] + [(y ^ b, xl ^ e, 1) for b in (1, 3) for e in range(2)]
    return [(y ^ b, xl, 0) for b in range(4)] + [(y ^ 2, xl ^ e, 1) for e in range(2)]


def part_kernel(part, count, *refs):
    mine, theirs = refs[0:count], refs[count : 2 * count]
    folded, out_ref, blocks, stored = refs[2 * count], *refs[-3:]
    y, z, xl, core = (lax.axis_index(name) for name in ("y", "z", "xl", "core"))
    half = 4 * F
    places = places_of(part, y, xl)

    def stores(i):
        return [
            pltpu.make_async_copy(blocks.at[i, n], out_ref.at[i, to_y, :, to_xl, to_core], stored.at[i, n])
            for n, (to_y, to_xl, to_core) in enumerate(places)
        ]

    def product(rows, columns):
        rows = rows[0] if len(rows) == 1 else jnp.concatenate(rows, axis=0)
        return lax.dot_general(rows, columns, (((1,), (1,)), ((), ())), preferred_element_type=jnp.float32)

    def compute(i, x_chunks, y_chunks):
        at = pl.ds(pl.multiple_of(2 * LAG * i, 2 * LAG), 2 * LAG)
        first, second = select(part, x_chunks, y_chunks)
        values = product(first, folded[at, :half]) + product(second, folded[at, half:])
        for n in range(len(places)):
            for g in range(NZ):
                blocks[i, n, z ^ g] = values[64 * n + 8 * g : 64 * n + 8 * g + 8]

    @pl.loop(0, 4)
    def _(i):
        @pl.when(core == 0)
        def _():
            compute(i, mine, theirs)

        @pl.when(core == 1)
        def _():
            compute(i, theirs, mine)

        for copy in stores(i):
            copy.start()

    @pl.loop(0, 4)
    def _(i):
        for copy in stores(i):
            copy.wait()


def correlate_part(part, mine, theirs, folded, out):
    count, blocks = len(mine), len(places_of(part, 0, 0))
    vmem = pl.BlockSpec(memory_space=pltpu.VMEM)
    hbm = pl.BlockSpec(memory_space=pltpu.HBM)
    operands = [*mine, *theirs, folded] + ([] if out is None else [out])
    return pl.pallas_call(
        functools.partial(part_kernel, part, count),
        in_specs=[vmem] * (2 * count + 1) + ([] if out is None else [hbm]),
        out_specs=hbm,
        out_shape=jax.ShapeDtypeStruct((4, NY, NZ, 2, 2, 8, 2 * LAG), jnp.float32),
        scratch_shapes=[
            pltpu.VMEM((4, blocks, NZ, 8, 2 * LAG), jnp.float32),
            pltpu.SemaphoreType.DMA((4, blocks)),
        ],
        input_output_aliases={} if out is None else {2 * count + 1: 0},
        cost_estimate=pl.CostEstimate(flops=2**20, bytes_accessed=2**10, transcendentals=0),
        compiler_params=pltpu.CompilerParams(vmem_limit_bytes=24 * 2**20),
        name="correlate",
    )(*operands)


def local(traces, lengths, mask):
    own = whiten(traces, lengths, mask)
    other = permute(own, other_group)
    ring = jnp.concatenate([own, permute(own, along_z(1))], axis=0)
    ring = jnp.concatenate([ring] + [permute(ring, along_z(d)) for d in (2, 4, 6)], axis=0)
    ring, own, other = lax.optimization_barrier((ring, own, other))
    plane = jnp.concatenate([ring] + [permute(ring, along_first(d)) for d in range(1, 4)], axis=0)
    folded = fold(own, other)
    plane, folded = lax.optimization_barrier((plane, folded))
    chunk1, chunk3 = permute(plane, along_second(1)), permute(plane, along_second(3))
    plane_too = permute(plane, other_core)
    out = correlate_part(0, [plane], [plane_too], folded, None)
    chunk1, chunk3, out, folded = lax.optimization_barrier((chunk1, chunk3, out, folded))
    top, bottom = permute(chunk3[:128], along_second(1)), permute(chunk1[128:], along_second(3))
    mine = [chunk1, chunk3]
    out = correlate_part(1, mine, [permute(chunk, other_core) for chunk in mine], folded, out)
    top, bottom, out = lax.optimization_barrier((top, bottom, out))
    theirs = [plane_too, permute(top, other_core), permute(bottom, other_core)]
    out = correlate_part(2, [plane, top, bottom], theirs, folded, out)
    return out.reshape(4, NY * NZ * 4 * 8, 2 * LAG)


def solution(mesh):
    finer = Mesh(mesh.devices.reshape(NY, NZ, 2, 2, 2), AXES)
    chan = ("y", "z", "xl", "core")
    return jax.shard_map(
        local,
        mesh=finer,
        in_specs=(P("tm", chan, None), P(), P(chan)),
        out_specs=P(AXES, None, None),
        check_vma=False,
    )
```

```python
import functools
import math

import jax
import jax.numpy as jnp
import ml_dtypes
import numpy as np
from jax import lax
from jax.experimental import pallas as pl
from jax.experimental.pallas import tpu as pltpu
from jax.sharding import Mesh
from jax.sharding import PartitionSpec as P

NFFT = 1024
LAG = 128
F = 512
SEG = 768
SUBWIN = 4
NY, NZ, NX = 4, 8, 4
AXES = ("y", "z", "xl", "core", "tm")


def dft_tables():
    product = np.mod(np.arange(SEG)[:, None] * np.arange(F)[None, :], NFFT)
    theta = product * (2.0 * math.pi / NFFT)
    table = np.concatenate([np.cos(theta), -np.sin(theta)], axis=1)
    high = table.astype(ml_dtypes.bfloat16)
    low = (table - high.astype(np.float64)).astype(ml_dtypes.bfloat16)
    return high, low


def lag_table():
    product = np.mod(np.arange(F)[:, None] * (np.arange(2 * LAG) - LAG)[None, :], NFFT)
    phase = product * (2.0 * math.pi / NFFT)
    weight = np.where(np.arange(F) == 0, 1.0, 2.0)[:, None] / math.sqrt(F * SUBWIN)
    table = np.concatenate([weight * np.cos(phase), -weight * np.sin(phase)], axis=0)
    return table.astype(np.float32).astype(ml_dtypes.bfloat16)


def device_index(y, z, x, core):
    return (((y * NZ + z) * 2 + x % 2) * 2 + core) * 2 + x // 2


def permute(value, partner):
    pairs = []
    for y in range(NY):
        for z in range(NZ):
            for x in range(NX):
                for core in range(2):
                    pairs.append((device_index(y, z, x, core), device_index(*partner(y, z, x, core))))
    return lax.ppermute(value, AXES, pairs)


def along_z(d):
    return lambda y, z, x, core: (y, z ^ d, x, core)


def along_first(d):
    return lambda y, z, x, core: (y ^ d, z, x, core) if core == 0 else (y, z, x ^ d, core)


def along_second(d):
    return lambda y, z, x, core: (y, z, x ^ d, core) if core == 0 else (y ^ d, z, x, core)


def other_core(y, z, x, core):
    return (y, z, x, 1 - core)


def other_group(y, z, x, core):
    return (y, z, x ^ 2, core)


def touch_kernel(high_ref, low_ref, out_ref):
    out_ref[...] = high_ref[0:16, 0:128] + low_ref[0:16, 0:128]


def touch(tables):
    vmem = pl.BlockSpec(memory_space=pltpu.VMEM)
    return pl.pallas_call(
        touch_kernel,
        in_specs=[vmem, vmem],
        out_specs=vmem,
        out_shape=jax.ShapeDtypeStruct((16, 128), jnp.bfloat16),
        cost_estimate=pl.CostEstimate(flops=2**10, bytes_accessed=2**10, transcendentals=0),
        compiler_params=pltpu.CompilerParams(vmem_limit_bytes=16 * 2**20),
        name="touch",
    )(*tables)


def whiten_kernel(lengths_ref, own_mask_ref, near_mask_ref, own_ref, near_ref, high_ref, low_ref, touched_ref, pair_ref, out_ref):
    del touched_ref
    tm = lax.axis_index("tm")
    x = jnp.concatenate([own_ref[...].reshape(16, SEG), near_ref[...].reshape(16, SEG)], axis=0)
    row = lax.broadcasted_iota(jnp.int32, (32, 1), 0)
    length = jnp.where(row % 16 < 8, lengths_ref[2 * tm], lengths_ref[2 * tm + 1])
    usable = jnp.zeros((32, 1), jnp.float32)
    for c in range(8):
        mask = jnp.where(row < 16, own_mask_ref[c], near_mask_ref[c])
        usable = jnp.where(row % 8 == c, mask.astype(jnp.float32), usable)
    live = lax.broadcasted_iota(jnp.int32, (32, SEG), 1) < length
    average = jnp.sum(jnp.where(live, x, 0.0), axis=1, keepdims=True) / length.astype(jnp.float32)
    centred = jnp.where(live, x - average, 0.0)
    part0 = centred.astype(jnp.bfloat16)
    rest = centred - part0.astype(jnp.float32)
    part1 = rest.astype(jnp.bfloat16)
    part2 = (rest - part1.astype(jnp.float32)).astype(jnp.bfloat16)
    parts = jnp.concatenate([part0, part1, part2], axis=0)
    by_high = jnp.dot(parts, high_ref[...], preferred_element_type=jnp.float32)
    by_low = jnp.dot(parts[:64], low_ref[...], preferred_element_type=jnp.float32)
    spectrum = by_high[:32] + (by_high[32:64] + by_low[:32] + (by_high[64:] + by_low[32:]))
    re, im = spectrum[:, :F], spectrum[:, F:]
    power = re * re + im * im
    level = jnp.mean(power, axis=1, keepdims=True)
    factor = usable / jnp.sqrt(power + 0.01 * level + 1e-06)
    white = [re * factor, im * factor]
    for k in range(2):
        for part in range(2):
            lanes = slice((2 * k + part) * F, (2 * k + part + 1) * F)
            own = white[part][8 * k : 8 * k + 8]
            pair_ref[:, lanes] = jnp.concatenate([own, white[part][16 + 8 * k : 24 + 8 * k]], axis=0).astype(jnp.bfloat16)
            out_ref[:, lanes] = own.astype(jnp.bfloat16)


def whiten(lengths, own_mask, near_mask, own, near, tables, touched):
    smem = pl.BlockSpec(memory_space=pltpu.SMEM)
    vmem = pl.BlockSpec(memory_space=pltpu.VMEM)
    return pl.pallas_call(
        whiten_kernel,
        in_specs=[smem, smem, smem, vmem, vmem, vmem, vmem, vmem],
        out_specs=[vmem, vmem],
        out_shape=[jax.ShapeDtypeStruct((rows, 4 * F), jnp.bfloat16) for rows in (16, 8)],
        compiler_params=pltpu.CompilerParams(vmem_limit_bytes=16 * 2**20),
        name="whiten",
    )(lengths, own_mask, near_mask, own, near, *tables, touched)


def fold_kernel(own_ref, other_ref, lag_ref, out_ref, rows):
    i = pl.program_id(0)
    rows[0] = own_ref[...].astype(jnp.float32)
    rows[1] = other_ref[...].astype(jnp.float32)
    mine = 4 * lax.axis_index("tm") + i
    step = 32

    @pl.loop(0, 2 * LAG, step=step)
    def _(begin):
        at = pl.ds(pl.multiple_of(begin, step), step)
        cos = lag_ref[at, :F].astype(jnp.float32)
        sin = lag_ref[at, F:].astype(jnp.float32)
        for group in range(2):
            for k in range(2):
                to = 2 * F * (2 * group + k)
                a_re = rows[group, pl.ds(mine, 1), 2 * k * F : (2 * k + 1) * F]
                a_im = rows[group, pl.ds(mine, 1), (2 * k + 1) * F : (2 * k + 2) * F]
                out_ref[at, to : to + F] = (a_re * cos + a_im * sin).astype(jnp.bfloat16)
                out_ref[at, to + F : to + 2 * F] = (a_im * cos - a_re * sin).astype(jnp.bfloat16)


def fold(own, other):
    whole = pl.BlockSpec((8, 4 * F), lambda i: (0, 0))
    return pl.pallas_call(
        fold_kernel,
        grid=(4,),
        in_specs=[whole, whole, pl.BlockSpec((2 * LAG, 2 * F), lambda i: (0, 0))],
        out_specs=pl.BlockSpec((2 * LAG, 8 * F), lambda i: (i, 0)),
        out_shape=jax.ShapeDtypeStruct((8 * LAG, 8 * F), jnp.bfloat16),
        scratch_shapes=[pltpu.VMEM((2, 8, 4 * F), jnp.float32)],
        cost_estimate=pl.CostEstimate(flops=2**20, bytes_accessed=2**10, transcendentals=0),
        compiler_params=pltpu.CompilerParams(vmem_limit_bytes=16 * 2**20),
        name="fold",
    )(own, other, jnp.asarray(np.ascontiguousarray(lag_table().T)))


ALL, TOP, BOTTOM = slice(0, 256), slice(0, 128), slice(128, 256)
NEAR = {
    0: ([(0, ALL)], [(1, ALL)], [(b, 1) for b in range(4)]),
    1: ([(0, TOP), (1, TOP)], [(0, BOTTOM), (1, BOTTOM)], [(1, 0), (1, 1), (3, 0), (3, 1)]),
}
FAR = {
    0: ([(0, ALL)], [(1, TOP), (2, TOP)], [(b, 0) for b in range(4)]),
    1: ([(0, TOP), (1, TOP)], [(0, BOTTOM), (2, TOP)], [(0, 0), (0, 1), (2, 0), (2, 1)]),
}


def part_kernel(work, count, *refs):
    chunks, folded, out_ref, blocks, stored = refs[:count], refs[count], *refs[-3:]
    y, z, xl, core = (lax.axis_index(name) for name in ("y", "z", "xl", "core"))
    half = 4 * F

    def rows_of(mine, pieces):
        rows = [mine[p][at, :] for p, at in pieces]
        return rows[0] if len(rows) == 1 else jnp.concatenate(rows, axis=0)

    def product(rows, columns):
        return lax.dot_general(rows, columns, (((1,), (1,)), ((), ())), preferred_element_type=jnp.float32)

    def run(kind, operands, job):
        first, second, offsets = job
        mine = [chunks[p] for p in operands]
        copies = []
        for i in range(4):
            at = slice(2 * LAG * i, 2 * LAG * (i + 1))
            values = product(rows_of(mine, first), folded[at, :half]) + product(rows_of(mine, second), folded[at, half:])
            for n, (dy, dxl) in enumerate(offsets):
                for g in range(NZ):
                    blocks[i, n, z ^ g] = values[64 * n + 8 * g : 64 * n + 8 * g + 8]
                copy = pltpu.make_async_copy(blocks.at[i, n], out_ref.at[i, y ^ dy, :, xl ^ dxl, kind], stored.at[i, n])
                copy.start()
                copies.append(copy)
        for copy in copies:
            copy.wait()

    for to_core in range(2):

        @pl.when(core == to_core)
        def _():
            run(*work[to_core])


def correlate_part(work, chunks, folded, out):
    count = len(chunks)
    blocks = max(len(job[2]) for _, _, job in work)
    vmem = pl.BlockSpec(memory_space=pltpu.VMEM)
    hbm = pl.BlockSpec(memory_space=pltpu.HBM)
    operands = [*chunks, folded] + ([] if out is None else [out])
    return pl.pallas_call(
        functools.partial(part_kernel, work, count),
        in_specs=[vmem] * (count + 1) + ([] if out is None else [hbm]),
        out_specs=hbm,
        out_shape=jax.ShapeDtypeStruct((4, NY, NZ, 2, 2, 8, 2 * LAG), jnp.float32),
        scratch_shapes=[
            pltpu.VMEM((4, blocks, NZ, 8, 2 * LAG), jnp.float32),
            pltpu.SemaphoreType.DMA((4, blocks)),
        ],
        input_output_aliases={} if out is None else {count + 1: 0},
        cost_estimate=pl.CostEstimate(flops=2**20, bytes_accessed=2**10, transcendentals=0),
        compiler_params=pltpu.CompilerParams(vmem_limit_bytes=24 * 2**20),
        name="correlate",
    )(*operands)


def of_own_class(part, chunks, folded, out):
    return correlate_part([(k, range(len(chunks)), part[k]) for k in (0, 1)], chunks, folded, out)


def of_other_class(part, chunks, folded, out):
    return correlate_part([(k, range(len(chunks)), part[k]) for k in (1, 0)], chunks, folded, out)


def local(traces, lengths, mask):
    near_traces, near_mask = permute(traces, along_z(1)), permute(mask, along_z(1))
    tables = [jnp.asarray(table) for table in dft_tables()]
    near_traces, near_mask, touched = lax.optimization_barrier((near_traces, near_mask, touch(tables)))
    pair, own = whiten(lengths, mask, near_mask, traces, near_traces, tables, touched)
    ring = jnp.concatenate([pair] + [permute(pair, along_z(d)) for d in (2, 4, 6)], axis=0)
    ring, own = lax.optimization_barrier((ring, own))
    other = permute(own, other_group)
    plane = jnp.concatenate([ring] + [permute(ring, along_first(d)) for d in range(1, 4)], axis=0)
    plane, own, other = lax.optimization_barrier((plane, own, other))
    near = [permute(plane, along_second(1)), permute(plane, along_second(3))]
    folded = fold(own, other)
    near[0], near[1], plane, folded = lax.optimization_barrier((near[0], near[1], plane, folded))
    top, bottom = permute(near[1][:128], along_second(1)), permute(near[0][128:], along_second(3))
    near_too = [permute(chunk, other_core) for chunk in near]
    plane_too = permute(plane, other_core)
    out = of_own_class(NEAR, near, folded, None)
    out = of_other_class(NEAR, near_too, folded, out)
    top, bottom, plane_too, out = lax.optimization_barrier((top, bottom, plane_too, out))
    top_too, bottom_too = permute(top, other_core), permute(bottom, other_core)
    out = of_own_class(FAR, [plane, top, bottom], folded, out)
    out = of_other_class(FAR, [plane_too, top_too, bottom_too], folded, out)
    return out.reshape(4, NY * NZ * 4 * 8, 2 * LAG)


def solution(mesh):
    finer = Mesh(mesh.devices.reshape(NY, NZ, 2, 2, 2), AXES)
    chan = ("y", "z", "xl", "core")
    return jax.shard_map(
        local,
        mesh=finer,
        in_specs=(P("tm", chan, None), P(), P(chan)),
        out_specs=P(AXES, None, None),
        check_vma=False,
    )
```

```python
import functools
import math

import jax
import jax.numpy as jnp
import ml_dtypes
import numpy as np
from jax import lax
from jax.experimental import pallas as pl
from jax.experimental.pallas import tpu as pltpu
from jax.sharding import Mesh
from jax.sharding import PartitionSpec as P

NFFT = 1024
LAG = 128
F = 512
SEG = 768
SUBWIN = 4
NY, NZ, NX = 4, 8, 4
Z_ORDER = (0, 2, 1, 3, 6, 4, 7, 5)
AXES = ("y", "z", "xl", "core", "tm")


def dft_tables():
    product = np.mod(np.arange(SEG)[:, None] * np.arange(F)[None, :], NFFT)
    theta = product * (2.0 * math.pi / NFFT)
    table = np.concatenate([np.cos(theta), -np.sin(theta)], axis=1)
    high = table.astype(ml_dtypes.bfloat16)
    low = (table - high.astype(np.float64)).astype(ml_dtypes.bfloat16)
    return high, low


def lag_table():
    product = np.mod(np.arange(F)[:, None] * (np.arange(2 * LAG) - LAG)[None, :], NFFT)
    phase = product * (2.0 * math.pi / NFFT)
    weight = np.where(np.arange(F) == 0, 1.0, 2.0)[:, None] / math.sqrt(F * SUBWIN)
    table = np.concatenate([weight * np.cos(phase), -weight * np.sin(phase)], axis=0)
    return table.astype(np.float32).astype(ml_dtypes.bfloat16)


def device_index(y, z, x, core):
    return (((y * NZ + z) * 2 + x % 2) * 2 + core) * 2 + x // 2


def permute(value, partner):
    pairs = []
    for y in range(NY):
        for z in range(NZ):
            for x in range(NX):
                for core in range(2):
                    pairs.append((device_index(y, z, x, core), device_index(*partner(y, z, x, core))))
    return lax.ppermute(value, AXES, pairs)


def along_z(d):
    return lambda y, z, x, core: (y, z ^ d, x, core)


def along_first(d):
    return lambda y, z, x, core: (y ^ d, z, x, core) if core == 0 else (y, z, x ^ d, core)


def along_second(d):
    return lambda y, z, x, core: (y, z, x ^ d, core) if core == 0 else (y ^ d, z, x, core)


def other_core(y, z, x, core):
    return (y, z, x, 1 - core)


def other_group(y, z, x, core):
    return (y, z, x ^ 2, core)


def touch_kernel(high_ref, low_ref, out_ref):
    out_ref[...] = high_ref[0:16, 0:128] + low_ref[0:16, 0:128]


def touch(tables):
    vmem = pl.BlockSpec(memory_space=pltpu.VMEM)
    return pl.pallas_call(
        touch_kernel,
        in_specs=[vmem, vmem],
        out_specs=vmem,
        out_shape=jax.ShapeDtypeStruct((16, 128), jnp.bfloat16),
        cost_estimate=pl.CostEstimate(flops=2**10, bytes_accessed=2**10, transcendentals=0),
        compiler_params=pltpu.CompilerParams(vmem_limit_bytes=16 * 2**20),
        name="touch",
    )(*tables)


def whiten_kernel(lengths_ref, own_mask_ref, near_mask_ref, own_ref, near_ref, high_ref, low_ref, touched_ref, pair_ref, out_ref):
    del touched_ref
    tm = lax.axis_index("tm")
    x = jnp.concatenate([own_ref[...].reshape(16, SEG), near_ref[...].reshape(16, SEG)], axis=0)
    row = lax.broadcasted_iota(jnp.int32, (32, 1), 0)
    length = jnp.where(row % 16 < 8, lengths_ref[2 * tm], lengths_ref[2 * tm + 1])
    usable = jnp.zeros((32, 1), jnp.float32)
    for c in range(8):
        mask = jnp.where(row < 16, own_mask_ref[c], near_mask_ref[c])
        usable = jnp.where(row % 8 == c, mask.astype(jnp.float32), usable)
    live = lax.broadcasted_iota(jnp.int32, (32, SEG), 1) < length
    average = jnp.sum(jnp.where(live, x, 0.0), axis=1, keepdims=True) / length.astype(jnp.float32)
    centred = jnp.where(live, x - average, 0.0)
    part0 = centred.astype(jnp.bfloat16)
    rest = centred - part0.astype(jnp.float32)
    part1 = rest.astype(jnp.bfloat16)
    part2 = (rest - part1.astype(jnp.float32)).astype(jnp.bfloat16)
    parts = jnp.concatenate([part0, part1, part2], axis=0)
    by_high = jnp.dot(parts, high_ref[...], preferred_element_type=jnp.float32)
    by_low = jnp.dot(parts[:64], low_ref[...], preferred_element_type=jnp.float32)
    spectrum = by_high[:32] + (by_high[32:64] + by_low[:32] + (by_high[64:] + by_low[32:]))
    re, im = spectrum[:, :F], spectrum[:, F:]
    power = re * re + im * im
    level = jnp.mean(power, axis=1, keepdims=True)
    factor = usable / jnp.sqrt(power + 0.01 * level + 1e-06)
    white = [re * factor, im * factor]
    for k in range(2):
        for part in range(2):
            lanes = slice((2 * k + part) * F, (2 * k + part + 1) * F)
            own = white[part][8 * k : 8 * k + 8]
            pair_ref[:, lanes] = jnp.concatenate([own, white[part][16 + 8 * k : 24 + 8 * k]], axis=0).astype(jnp.bfloat16)
            out_ref[:, lanes] = own.astype(jnp.bfloat16)


def whiten(lengths, own_mask, near_mask, own, near, tables, touched):
    smem = pl.BlockSpec(memory_space=pltpu.SMEM)
    vmem = pl.BlockSpec(memory_space=pltpu.VMEM)
    return pl.pallas_call(
        whiten_kernel,
        in_specs=[smem, smem, smem, vmem, vmem, vmem, vmem, vmem],
        out_specs=[vmem, vmem],
        out_shape=[jax.ShapeDtypeStruct((rows, 4 * F), jnp.bfloat16) for rows in (16, 8)],
        compiler_params=pltpu.CompilerParams(vmem_limit_bytes=16 * 2**20),
        name="whiten",
    )(lengths, own_mask, near_mask, own, near, *tables, touched)


def fold_kernel(own_ref, other_ref, lag_ref, out_ref, rows):
    i = pl.program_id(0)
    rows[0] = own_ref[...].astype(jnp.float32)
    rows[1] = other_ref[...].astype(jnp.float32)
    mine = 4 * lax.axis_index("tm") + i
    step = 32

    @pl.loop(0, 2 * LAG, step=step)
    def _(begin):
        at = pl.ds(pl.multiple_of(begin, step), step)
        cos = lag_ref[at, :F].astype(jnp.float32)
        sin = lag_ref[at, F:].astype(jnp.float32)
        for group in range(2):
            for k in range(2):
                to = 2 * F * (2 * group + k)
                a_re = rows[group, pl.ds(mine, 1), 2 * k * F : (2 * k + 1) * F]
                a_im = rows[group, pl.ds(mine, 1), (2 * k + 1) * F : (2 * k + 2) * F]
                out_ref[at, to : to + F] = (a_re * cos + a_im * sin).astype(jnp.bfloat16)
                out_ref[at, to + F : to + 2 * F] = (a_im * cos - a_re * sin).astype(jnp.bfloat16)


def fold(own, other):
    whole = pl.BlockSpec((8, 4 * F), lambda i: (0, 0))
    return pl.pallas_call(
        fold_kernel,
        grid=(4,),
        in_specs=[whole, whole, pl.BlockSpec((2 * LAG, 2 * F), lambda i: (0, 0))],
        out_specs=pl.BlockSpec((2 * LAG, 8 * F), lambda i: (i, 0)),
        out_shape=jax.ShapeDtypeStruct((8 * LAG, 8 * F), jnp.bfloat16),
        scratch_shapes=[pltpu.VMEM((2, 8, 4 * F), jnp.float32)],
        cost_estimate=pl.CostEstimate(flops=2**20, bytes_accessed=2**10, transcendentals=0),
        compiler_params=pltpu.CompilerParams(vmem_limit_bytes=16 * 2**20),
        name="fold",
    )(own, other, jnp.asarray(np.ascontiguousarray(lag_table().T)))


ALL, TOP, BOTTOM = slice(0, 256), slice(0, 128), slice(128, 256)
NEAR = {
    0: ([(0, ALL)], [(1, ALL)], [(b, 1) for b in range(4)]),
    1: ([(0, TOP), (1, TOP)], [(0, BOTTOM), (1, BOTTOM)], [(1, 0), (1, 1), (3, 0), (3, 1)]),
}
FAR = {
    0: (None, [(1, TOP), (2, TOP)], [(b, 0) for b in range(4)]),
    1: ([(0, TOP), (1, TOP)], [(0, BOTTOM), (2, TOP)], [(0, 0), (0, 1), (2, 0), (2, 1)]),
}


def part_kernel(work, earlier, has_early, last, count, *refs):
    refs = list(refs)
    chunks, folded = [refs.pop(0) for _ in range(count)], refs.pop(0)
    early = refs.pop(0) if has_early else None
    before = refs.pop(0) if earlier else None
    out_ref = refs.pop(0) if earlier else None
    result, sent = refs
    y, z, xl, core = (lax.axis_index(name) for name in ("y", "z", "xl", "core"))
    half = 4 * F

    def product(mine, pieces, columns):
        rows = [mine[p][at, :] for p, at in pieces]
        rows = rows[0] if len(rows) == 1 else jnp.concatenate(rows, axis=0)
        return lax.dot_general(rows, columns, (((1,), (1,)), ((), ())), preferred_element_type=jnp.float32)

    def copies_of(source, kind, offsets, i, slot):
        return [
            pltpu.make_async_copy(source.at[i, n], out_ref.at[i, y ^ dy, :, xl ^ dxl, kind], sent.at[slot, i, n])
            for n, (dy, dxl) in enumerate(offsets)
        ]

    def run(c):
        copies = []
        if earlier:
            for i in range(4):
                copies += copies_of(before, earlier[c][0], earlier[c][1][2], i, 0)
        for copy in copies:
            copy.start()
        kind, (first, second, offsets) = work[c]
        for i in range(4):
            at = slice(2 * LAG * i, 2 * LAG * (i + 1))
            values = early[:, at] if first is None else product(chunks, first, folded[at, :half])
            values += product(chunks, second, folded[at, half:])
            for n in range(len(offsets)):
                for g in range(NZ):
                    result[i, n, z ^ Z_ORDER[g]] = values[64 * n + 8 * g : 64 * n + 8 * g + 8]
            if last:
                own = copies_of(result, kind, offsets, i, 1)
                for copy in own:
                    copy.start()
                copies += own
        for copy in copies:
            copy.wait()

    for c in range(2):

        @pl.when(core == c)
        def _():
            run(c)


RESULT = (4, 4, NZ, 8, 2 * LAG)
VMEM_SPEC = pl.BlockSpec(memory_space=pltpu.VMEM)
HBM_SPEC = pl.BlockSpec(memory_space=pltpu.HBM)
OUT = jax.ShapeDtypeStruct((4, NY, NZ, 2, 2, 8, 2 * LAG), jnp.float32)
SMALL = pl.CostEstimate(flops=2**20, bytes_accessed=2**10, transcendentals=0)


def correlate_part(work, chunks, folded, early=None, before=None, earlier=None, out=None, last=False):
    operands = [*chunks, folded] + [array for array in (early, before) if array is not None]
    in_specs = [VMEM_SPEC] * len(operands)
    aliases = {}
    if out is not None:
        aliases = {len(operands): 0}
        operands, in_specs = [*operands, out], [*in_specs, HBM_SPEC]
    results = ([(HBM_SPEC, OUT)] if earlier else []) + (
        [] if last else [(VMEM_SPEC, jax.ShapeDtypeStruct(RESULT, jnp.float32))]
    )
    kernel = functools.partial(part_kernel, work, earlier, early is not None, last, len(chunks))
    return pl.pallas_call(
        kernel if out is None else lambda *refs: kernel(*refs[: len(operands) - 1], *refs[len(operands) :]),
        in_specs=in_specs,
        out_specs=[spec for spec, _ in results],
        out_shape=[shape for _, shape in results],
        scratch_shapes=([pltpu.VMEM(RESULT, jnp.float32)] if last else []) + [pltpu.SemaphoreType.DMA((2, 4, 4))],
        input_output_aliases=aliases,
        cost_estimate=SMALL,
        compiler_params=pltpu.CompilerParams(vmem_limit_bytes=24 * 2**20),
        name="correlate",
    )(*operands)


def plane_kernel(earlier, mine_ref, theirs_ref, folded, before, _, out_ref, early, sent):
    y, xl, core = (lax.axis_index(name) for name in ("y", "xl", "core"))

    def run(c, rows):
        kind, (_, _, offsets) = earlier[c]
        copies = [
            pltpu.make_async_copy(before.at[i, n], out_ref.at[i, y ^ dy, :, xl ^ dxl, kind], sent.at[i, n])
            for i in range(4)
            for n, (dy, dxl) in enumerate(offsets)
        ]
        for copy in copies:
            copy.start()
        early[...] = lax.dot_general(
            rows[...], folded[:, : 4 * F], (((1,), (1,)), ((), ())), preferred_element_type=jnp.float32
        )
        for copy in copies:
            copy.wait()

    for c in range(2):

        @pl.when(core == c)
        def _():
            run(c, (mine_ref, theirs_ref)[c])


def correlate_plane(mine, theirs, folded, before, earlier, out):
    return pl.pallas_call(
        functools.partial(plane_kernel, earlier),
        in_specs=[VMEM_SPEC] * 4 + [HBM_SPEC],
        out_specs=[HBM_SPEC, VMEM_SPEC],
        out_shape=[OUT, jax.ShapeDtypeStruct((256, 8 * LAG), jnp.float32)],
        scratch_shapes=[pltpu.SemaphoreType.DMA((4, 4))],
        input_output_aliases={4: 0},
        cost_estimate=SMALL,
        compiler_params=pltpu.CompilerParams(vmem_limit_bytes=24 * 2**20),
        name="plane",
    )(mine, theirs, folded, before, out)


def of_own_class(part):
    return [(kind, part[kind]) for kind in (0, 1)]


def of_other_class(part):
    return [(kind, part[kind]) for kind in (1, 0)]


def local(traces, lengths, mask):
    near_traces, near_mask = permute(traces, along_z(2)), permute(mask, along_z(2))
    tables = [jnp.asarray(table) for table in dft_tables()]
    near_traces, near_mask, touched = lax.optimization_barrier((near_traces, near_mask, touch(tables)))
    pair, own = whiten(lengths, mask, near_mask, traces, near_traces, tables, touched)
    ring = jnp.concatenate([pair] + [permute(pair, along_z(d)) for d in (1, 6, 7)], axis=0)
    ring, own = lax.optimization_barrier((ring, own))
    other = permute(own, other_group)
    plane = jnp.concatenate([ring] + [permute(ring, along_first(d)) for d in range(1, 4)], axis=0)
    plane, own, other = lax.optimization_barrier((plane, own, other))
    near = [permute(plane, along_second(1)), permute(plane, along_second(3))]
    folded = fold(own, other)
    near[0], near[1], plane, folded = lax.optimization_barrier((near[0], near[1], plane, folded))
    top, bottom = permute(near[1][:128], along_second(1)), permute(near[0][128:], along_second(3))
    near_too = [permute(chunk, other_core) for chunk in near]
    plane_too = permute(plane, other_core)
    (before,) = correlate_part(of_own_class(NEAR), near, folded)
    out, before = correlate_part(of_other_class(NEAR), near_too, folded, before=before, earlier=of_own_class(NEAR))
    plane, plane_too, before, out = lax.optimization_barrier((plane, plane_too, before, out))
    out, early = correlate_plane(plane, plane_too, folded, before, of_other_class(NEAR), out)
    top, bottom, out, early = lax.optimization_barrier((top, bottom, out, early))
    top_too, bottom_too = permute(top, other_core), permute(bottom, other_core)
    (before,) = correlate_part(of_own_class(FAR), [plane, top, bottom], folded, early)
    (out,) = correlate_part(
        of_other_class(FAR),
        [plane_too, top_too, bottom_too],
        folded,
        early,
        before=before,
        earlier=of_own_class(FAR),
        out=out,
        last=True,
    )
    return out.reshape(4, NY * NZ * 4 * 8, 2 * LAG)


def solution(mesh):
    finer = Mesh(mesh.devices.reshape(NY, NZ, 2, 2, 2), AXES)
    chan = ("y", "z", "xl", "core")
    return jax.shard_map(
        local,
        mesh=finer,
        in_specs=(P("tm", chan, None), P(), P(chan)),
        out_specs=P(AXES, None, None),
        check_vma=False,
    )
```

```python
import functools
import math

import jax
import jax.numpy as jnp
import ml_dtypes
import numpy as np
from jax import lax
from jax.experimental import pallas as pl
from jax.experimental.pallas import tpu as pltpu
from jax.sharding import Mesh
from jax.sharding import PartitionSpec as P

NFFT = 1024
LAG = 128
F = 512
SEG = 768
SUBWIN = 4
NY, NZ, NX = 4, 8, 4
Z_ORDER = (0, 2, 1, 3, 6, 4, 7, 5)
AXES = ("y", "z", "xl", "core", "tm")


def dft_tables():
    product = np.mod(np.arange(SEG)[:, None] * np.arange(F)[None, :], NFFT)
    theta = product * (2.0 * math.pi / NFFT)
    table = np.concatenate([np.cos(theta), -np.sin(theta)], axis=1)
    high = table.astype(ml_dtypes.bfloat16)
    low = (table - high.astype(np.float64)).astype(ml_dtypes.bfloat16)
    return high, low


def lag_table():
    product = np.mod(np.arange(F)[:, None] * (np.arange(2 * LAG) - LAG)[None, :], NFFT)
    phase = product * (2.0 * math.pi / NFFT)
    weight = np.where(np.arange(F) == 0, 1.0, 2.0)[:, None] / math.sqrt(F * SUBWIN)
    table = np.concatenate([weight * np.cos(phase), -weight * np.sin(phase)], axis=0)
    return table.astype(np.float32).astype(ml_dtypes.bfloat16)


def device_index(y, z, x, core):
    return (((y * NZ + z) * 2 + x % 2) * 2 + core) * 2 + x // 2


def permute(value, partner):
    pairs = []
    for y in range(NY):
        for z in range(NZ):
            for x in range(NX):
                for core in range(2):
                    pairs.append((device_index(y, z, x, core), device_index(*partner(y, z, x, core))))
    return lax.ppermute(value, AXES, pairs)


def along_z(d):
    return lambda y, z, x, core: (y, z ^ d, x, core)


def along_first(d):
    return lambda y, z, x, core: (y ^ d, z, x, core) if core == 0 else (y, z, x ^ d, core)


def along_second(d):
    return lambda y, z, x, core: (y, z, x ^ d, core) if core == 0 else (y ^ d, z, x, core)


def other_core(y, z, x, core):
    return (y, z, x, 1 - core)


def other_group(y, z, x, core):
    return (y, z, x ^ 2, core)


def touch_kernel(high_ref, low_ref, out_ref):
    out_ref[...] = high_ref[0:16, 0:128] + low_ref[0:16, 0:128]


def touch(tables):
    vmem = pl.BlockSpec(memory_space=pltpu.VMEM)
    return pl.pallas_call(
        touch_kernel,
        in_specs=[vmem, vmem],
        out_specs=vmem,
        out_shape=jax.ShapeDtypeStruct((16, 128), jnp.bfloat16),
        cost_estimate=pl.CostEstimate(flops=2**10, bytes_accessed=2**10, transcendentals=0),
        compiler_params=pltpu.CompilerParams(vmem_limit_bytes=16 * 2**20),
        name="touch",
    )(*tables)


def whiten_kernel(lengths_ref, own_mask_ref, near_mask_ref, own_ref, near_ref, high_ref, low_ref, touched_ref, pair_ref, out_ref):
    del touched_ref
    tm = lax.axis_index("tm")
    x = jnp.concatenate([own_ref[...].reshape(16, SEG), near_ref[...].reshape(16, SEG)], axis=0)
    row = lax.broadcasted_iota(jnp.int32, (32, 1), 0)
    length = jnp.where(row % 16 < 8, lengths_ref[2 * tm], lengths_ref[2 * tm + 1])
    usable = jnp.zeros((32, 1), jnp.float32)
    for c in range(8):
        mask = jnp.where(row < 16, own_mask_ref[c], near_mask_ref[c])
        usable = jnp.where(row % 8 == c, mask.astype(jnp.float32), usable)
    live = lax.broadcasted_iota(jnp.int32, (32, SEG), 1) < length
    average = jnp.sum(jnp.where(live, x, 0.0), axis=1, keepdims=True) / length.astype(jnp.float32)
    centred = jnp.where(live, x - average, 0.0)
    part0 = centred.astype(jnp.bfloat16)
    rest = centred - part0.astype(jnp.float32)
    part1 = rest.astype(jnp.bfloat16)
    part2 = (rest - part1.astype(jnp.float32)).astype(jnp.bfloat16)
    parts = jnp.concatenate([part0, part1, part2], axis=0)
    by_high = jnp.dot(parts, high_ref[...], preferred_element_type=jnp.float32)
    by_low = jnp.dot(parts[:64], low_ref[...], preferred_element_type=jnp.float32)
    spectrum = by_high[:32] + (by_high[32:64] + by_low[:32] + (by_high[64:] + by_low[32:]))
    re, im = spectrum[:, :F], spectrum[:, F:]
    power = re * re + im * im
    level = jnp.mean(power, axis=1, keepdims=True)
    factor = usable / jnp.sqrt(power + 0.01 * level + 1e-06)
    white = [re * factor, im * factor]
    for k in range(2):
        for part in range(2):
            lanes = slice((2 * k + part) * F, (2 * k + part + 1) * F)
            own = white[part][8 * k : 8 * k + 8]
            pair_ref[:, lanes] = jnp.concatenate([own, white[part][16 + 8 * k : 24 + 8 * k]], axis=0).astype(jnp.bfloat16)
            out_ref[:, lanes] = own.astype(jnp.bfloat16)


def whiten(lengths, own_mask, near_mask, own, near, tables, touched):
    smem = pl.BlockSpec(memory_space=pltpu.SMEM)
    vmem = pl.BlockSpec(memory_space=pltpu.VMEM)
    return pl.pallas_call(
        whiten_kernel,
        in_specs=[smem, smem, smem, vmem, vmem, vmem, vmem, vmem],
        out_specs=[vmem, vmem],
        out_shape=[jax.ShapeDtypeStruct((rows, 4 * F), jnp.bfloat16) for rows in (16, 8)],
        compiler_params=pltpu.CompilerParams(vmem_limit_bytes=16 * 2**20),
        name="whiten",
    )(lengths, own_mask, near_mask, own, near, *tables, touched)


def fold_kernel(own_ref, other_ref, lag_ref, out_ref, rows):
    i = pl.program_id(0)
    rows[0] = own_ref[...].astype(jnp.float32)
    rows[1] = other_ref[...].astype(jnp.float32)
    mine = 4 * lax.axis_index("tm") + i
    step = 32

    @pl.loop(0, 2 * LAG, step=step)
    def _(begin):
        at = pl.ds(pl.multiple_of(begin, step), step)
        cos = lag_ref[at, :F].astype(jnp.float32)
        sin = lag_ref[at, F:].astype(jnp.float32)
        for group in range(2):
            for k in range(2):
                to = 2 * F * (2 * group + k)
                a_re = rows[group, pl.ds(mine, 1), 2 * k * F : (2 * k + 1) * F]
                a_im = rows[group, pl.ds(mine, 1), (2 * k + 1) * F : (2 * k + 2) * F]
                out_ref[at, to : to + F] = (a_re * cos + a_im * sin).astype(jnp.bfloat16)
                out_ref[at, to + F : to + 2 * F] = (a_im * cos - a_re * sin).astype(jnp.bfloat16)


def fold(own, other):
    whole = pl.BlockSpec((8, 4 * F), lambda i: (0, 0))
    return pl.pallas_call(
        fold_kernel,
        grid=(4,),
        in_specs=[whole, whole, pl.BlockSpec((2 * LAG, 2 * F), lambda i: (0, 0))],
        out_specs=pl.BlockSpec((2 * LAG, 8 * F), lambda i: (i, 0)),
        out_shape=jax.ShapeDtypeStruct((8 * LAG, 8 * F), jnp.bfloat16),
        scratch_shapes=[pltpu.VMEM((2, 8, 4 * F), jnp.float32)],
        cost_estimate=pl.CostEstimate(flops=2**20, bytes_accessed=2**10, transcendentals=0),
        compiler_params=pltpu.CompilerParams(vmem_limit_bytes=16 * 2**20),
        name="fold",
    )(own, other, jnp.asarray(np.ascontiguousarray(lag_table().T)))


ALL, TOP, BOTTOM = slice(0, 256), slice(0, 128), slice(128, 256)
NEAR = {
    0: ([(0, TOP), (1, TOP)], [(2, TOP), (3, TOP)], [(b, 1) for b in range(4)]),
    1: ([(0, TOP), (2, TOP)], [(1, TOP), (3, TOP)], [(1, 0), (1, 1), (3, 0), (3, 1)]),
}
FAR = {
    0: (None, [(2, TOP), (3, TOP)], [(b, 0) for b in range(4)]),
    1: ([(0, TOP), (2, TOP)], [(1, TOP), (3, TOP)], [(0, 0), (0, 1), (2, 0), (2, 1)]),
}


def part_kernel(work, earlier, has_early, last, count, *refs):
    refs = list(refs)
    chunks, folded = [refs.pop(0) for _ in range(count)], refs.pop(0)
    early = refs.pop(0) if has_early else None
    before = refs.pop(0) if earlier else None
    out_ref = refs.pop(0) if earlier else None
    result, sent = refs
    y, z, xl, core = (lax.axis_index(name) for name in ("y", "z", "xl", "core"))
    half = 4 * F

    def product(mine, pieces, columns):
        rows = [mine[p][at, :] for p, at in pieces]
        rows = rows[0] if len(rows) == 1 else jnp.concatenate(rows, axis=0)
        return lax.dot_general(rows, columns, (((1,), (1,)), ((), ())), preferred_element_type=jnp.float32)

    def copies_of(source, kind, offsets, i, slot):
        return [
            pltpu.make_async_copy(source.at[i, n], out_ref.at[i, y ^ dy, :, xl ^ dxl, kind], sent.at[slot, i, n])
            for n, (dy, dxl) in enumerate(offsets)
        ]

    def run(c):
        copies = []
        if earlier:
            for i in range(4):
                copies += copies_of(before, earlier[c][0], earlier[c][1][2], i, 0)
        for copy in copies:
            copy.start()
        kind, (first, second, offsets) = work[c]
        for i in range(4):
            at = slice(2 * LAG * i, 2 * LAG * (i + 1))
            values = early[:, at] if first is None else product(chunks, first, folded[at, :half])
            values += product(chunks, second, folded[at, half:])
            for n in range(len(offsets)):
                for g in range(NZ):
                    result[i, n, z ^ Z_ORDER[g]] = values[64 * n + 8 * g : 64 * n + 8 * g + 8]
            if last:
                own = copies_of(result, kind, offsets, i, 1)
                for copy in own:
                    copy.start()
                copies += own
        for copy in copies:
            copy.wait()

    for c in range(2):

        @pl.when(core == c)
        def _():
            run(c)


RESULT = (4, 4, NZ, 8, 2 * LAG)
VMEM_SPEC = pl.BlockSpec(memory_space=pltpu.VMEM)
HBM_SPEC = pl.BlockSpec(memory_space=pltpu.HBM)
OUT = jax.ShapeDtypeStruct((4, NY, NZ, 2, 2, 8, 2 * LAG), jnp.float32)
SMALL = pl.CostEstimate(flops=2**20, bytes_accessed=2**10, transcendentals=0)


def correlate_part(work, chunks, folded, early=None, before=None, earlier=None, out=None, last=False):
    operands = [*chunks, folded] + [array for array in (early, before) if array is not None]
    in_specs = [VMEM_SPEC] * len(operands)
    aliases = {}
    if out is not None:
        aliases = {len(operands): 0}
        operands, in_specs = [*operands, out], [*in_specs, HBM_SPEC]
    results = ([(HBM_SPEC, OUT)] if earlier else []) + (
        [] if last else [(VMEM_SPEC, jax.ShapeDtypeStruct(RESULT, jnp.float32))]
    )
    kernel = functools.partial(part_kernel, work, earlier, early is not None, last, len(chunks))
    return pl.pallas_call(
        kernel if out is None else lambda *refs: kernel(*refs[: len(operands) - 1], *refs[len(operands) :]),
        in_specs=in_specs,
        out_specs=[spec for spec, _ in results],
        out_shape=[shape for _, shape in results],
        scratch_shapes=([pltpu.VMEM(RESULT, jnp.float32)] if last else []) + [pltpu.SemaphoreType.DMA((2, 4, 4))],
        input_output_aliases=aliases,
        cost_estimate=SMALL,
        compiler_params=pltpu.CompilerParams(vmem_limit_bytes=24 * 2**20),
        name="correlate",
    )(*operands)


def plane_kernel(earlier, top, bottom, top_too, bottom_too, folded, before, _, out_ref, early, sent):
    y, xl, core = (lax.axis_index(name) for name in ("y", "xl", "core"))

    def run(c, rows):
        kind, (_, _, offsets) = earlier[c]
        copies = [
            pltpu.make_async_copy(before.at[i, n], out_ref.at[i, y ^ dy, :, xl ^ dxl, kind], sent.at[i, n])
            for i in range(4)
            for n, (dy, dxl) in enumerate(offsets)
        ]
        for copy in copies:
            copy.start()
        early[...] = lax.dot_general(
            jnp.concatenate([half[...] for half in rows], axis=0),
            folded[:, : 4 * F],
            (((1,), (1,)), ((), ())),
            preferred_element_type=jnp.float32,
        )
        for copy in copies:
            copy.wait()

    for c in range(2):

        @pl.when(core == c)
        def _():
            run(c, ((top, bottom), (top_too, bottom_too))[c])


def correlate_plane(mine, theirs, folded, before, earlier, out):
    return pl.pallas_call(
        functools.partial(plane_kernel, earlier),
        in_specs=[VMEM_SPEC] * 6 + [HBM_SPEC],
        out_specs=[HBM_SPEC, VMEM_SPEC],
        out_shape=[OUT, jax.ShapeDtypeStruct((256, 8 * LAG), jnp.float32)],
        scratch_shapes=[pltpu.SemaphoreType.DMA((4, 4))],
        input_output_aliases={6: 0},
        cost_estimate=SMALL,
        compiler_params=pltpu.CompilerParams(vmem_limit_bytes=24 * 2**20),
        name="plane",
    )(*mine, *theirs, folded, before, out)


def of_own_class(part):
    return [(kind, part[kind]) for kind in (0, 1)]


def of_other_class(part):
    return [(kind, part[kind]) for kind in (1, 0)]


def local(traces, lengths, mask):
    near_traces, near_mask = permute(traces, along_z(2)), permute(mask, along_z(2))
    tables = [jnp.asarray(table) for table in dft_tables()]
    near_traces, near_mask, touched = lax.optimization_barrier((near_traces, near_mask, touch(tables)))
    pair, own = whiten(lengths, mask, near_mask, traces, near_traces, tables, touched)
    ring = jnp.concatenate([pair] + [permute(pair, along_z(d)) for d in (1, 6, 7)], axis=0)
    ring, own = lax.optimization_barrier((ring, own))
    other = permute(own, other_group)
    first = [permute(ring, along_first(d)) for d in range(1, 4)]
    top = jnp.concatenate([ring, first[0]], axis=0)
    bottom, own, other = lax.optimization_barrier((jnp.concatenate(first[1:], axis=0), own, other))
    near_bottom = [permute(bottom, along_second(d)) for d in (1, 3)]
    near_top = [permute(top, along_second(d)) for d in (1, 3)]
    folded = fold(own, other)
    near = [near_top[0], near_bottom[0], near_top[1], near_bottom[1]]
    *near, top, bottom, folded = lax.optimization_barrier((*near, top, bottom, folded))
    near_too = [permute(half, other_core) for half in near]
    plane = [top, bottom]
    plane_too = [permute(half, other_core) for half in plane]
    far = [permute(near[2], along_second(1)), permute(near[1], along_second(3))]
    (before,) = correlate_part(of_own_class(NEAR), near, folded)
    out, before = correlate_part(of_other_class(NEAR), near_too, folded, before=before, earlier=of_own_class(NEAR))
    plane_too[0], plane_too[1], before, out = lax.optimization_barrier((*plane_too, before, out))
    out, early = correlate_plane(plane, plane_too, folded, before, of_other_class(NEAR), out)
    far[0], far[1], out, early = lax.optimization_barrier((*far, out, early))
    far_too = [permute(half, other_core) for half in far]
    (before,) = correlate_part(of_own_class(FAR), [*plane, *far], folded, early)
    (out,) = correlate_part(
        of_other_class(FAR),
        [*plane_too, *far_too],
        folded,
        early,
        before=before,
        earlier=of_own_class(FAR),
        out=out,
        last=True,
    )
    return out.reshape(4, NY * NZ * 4 * 8, 2 * LAG)


def solution(mesh):
    finer = Mesh(mesh.devices.reshape(NY, NZ, 2, 2, 2), AXES)
    chan = ("y", "z", "xl", "core")
    return jax.shard_map(
        local,
        mesh=finer,
        in_specs=(P("tm", chan, None), P(), P(chan)),
        out_specs=P(AXES, None, None),
        check_vma=False,
    )
```

```python
import functools
import math

import jax
import jax.numpy as jnp
import ml_dtypes
import numpy as np
from jax import lax
from jax.experimental import pallas as pl
from jax.experimental.pallas import tpu as pltpu
from jax.sharding import Mesh
from jax.sharding import PartitionSpec as P

NFFT = 1024
LAG = 128
F = 512
SEG = 768
SUBWIN = 4
NY, NZ, NX = 4, 8, 4
Z_ORDER = (0, 2, 1, 3, 6, 4, 7, 5)
AXES = ("y", "z", "xl", "core", "tm")


def dft_tables():
    product = np.mod(np.arange(SEG)[:, None] * np.arange(F)[None, :], NFFT)
    theta = product * (2.0 * math.pi / NFFT)
    table = np.concatenate([np.cos(theta), -np.sin(theta)], axis=1)
    high = table.astype(ml_dtypes.bfloat16)
    low = (table - high.astype(np.float64)).astype(ml_dtypes.bfloat16)
    return high, low


def lag_table():
    product = np.mod(np.arange(F)[:, None] * (np.arange(2 * LAG) - LAG)[None, :], NFFT)
    phase = product * (2.0 * math.pi / NFFT)
    weight = np.where(np.arange(F) == 0, 1.0, 2.0)[:, None] / math.sqrt(F * SUBWIN)
    table = np.concatenate([weight * np.cos(phase), -weight * np.sin(phase)], axis=0)
    return table.astype(np.float32).astype(ml_dtypes.bfloat16)


def device_index(y, z, x, core):
    return (((y * NZ + z) * 2 + x % 2) * 2 + core) * 2 + x // 2


def permute(value, partner):
    pairs = []
    for y in range(NY):
        for z in range(NZ):
            for x in range(NX):
                for core in range(2):
                    pairs.append((device_index(y, z, x, core), device_index(*partner(y, z, x, core))))
    return lax.ppermute(value, AXES, pairs)


def along_z(d):
    return lambda y, z, x, core: (y, z ^ d, x, core)


def along_first(d):
    return lambda y, z, x, core: (y ^ d, z, x, core) if core == 0 else (y, z, x ^ d, core)


def along_second(d):
    return lambda y, z, x, core: (y, z, x ^ d, core) if core == 0 else (y ^ d, z, x, core)


def other_core(y, z, x, core):
    return (y, z, x, 1 - core)


def other_group(y, z, x, core):
    return (y, z, x ^ 2, core)


def touch_kernel(high_ref, low_ref, out_ref):
    out_ref[...] = high_ref[0:16, 0:128] + low_ref[0:16, 0:128]


def touch(tables):
    vmem = pl.BlockSpec(memory_space=pltpu.VMEM)
    return pl.pallas_call(
        touch_kernel,
        in_specs=[vmem, vmem],
        out_specs=vmem,
        out_shape=jax.ShapeDtypeStruct((16, 128), jnp.bfloat16),
        cost_estimate=pl.CostEstimate(flops=2**10, bytes_accessed=2**10, transcendentals=0),
        compiler_params=pltpu.CompilerParams(vmem_limit_bytes=16 * 2**20),
        name="touch",
    )(*tables)


def whiten_kernel(lengths_ref, own_mask_ref, near_mask_ref, own_ref, near_ref, high_ref, low_ref, touched_ref, pair_ref, out_ref):
    del touched_ref
    tm = lax.axis_index("tm")
    x = jnp.concatenate([own_ref[...].reshape(16, SEG), near_ref[...].reshape(16, SEG)], axis=0)
    row = lax.broadcasted_iota(jnp.int32, (32, 1), 0)
    length = jnp.where(row % 16 < 8, lengths_ref[2 * tm], lengths_ref[2 * tm + 1])
    usable = jnp.zeros((32, 1), jnp.float32)
    for c in range(8):
        mask = jnp.where(row < 16, own_mask_ref[c], near_mask_ref[c])
        usable = jnp.where(row % 8 == c, mask.astype(jnp.float32), usable)
    live = lax.broadcasted_iota(jnp.int32, (32, SEG), 1) < length
    average = jnp.sum(jnp.where(live, x, 0.0), axis=1, keepdims=True) / length.astype(jnp.float32)
    centred = jnp.where(live, x - average, 0.0)
    part0 = centred.astype(jnp.bfloat16)
    rest = centred - part0.astype(jnp.float32)
    part1 = rest.astype(jnp.bfloat16)
    part2 = (rest - part1.astype(jnp.float32)).astype(jnp.bfloat16)
    parts = jnp.concatenate([part0, part1, part2], axis=0)
    by_high = jnp.dot(parts, high_ref[...], preferred_element_type=jnp.float32)
    by_low = jnp.dot(parts[:64], low_ref[...], preferred_element_type=jnp.float32)
    spectrum = by_high[:32] + (by_high[32:64] + by_low[:32] + (by_high[64:] + by_low[32:]))
    re, im = spectrum[:, :F], spectrum[:, F:]
    power = re * re + im * im
    level = jnp.mean(power, axis=1, keepdims=True)
    factor = usable / jnp.sqrt(power + 0.01 * level + 1e-06)
    white = [re * factor, im * factor]
    for k in range(2):
        for part in range(2):
            lanes = slice((2 * k + part) * F, (2 * k + part + 1) * F)
            own = white[part][8 * k : 8 * k + 8]
            pair_ref[:, lanes] = jnp.concatenate([own, white[part][16 + 8 * k : 24 + 8 * k]], axis=0).astype(jnp.bfloat16)
            out_ref[:, lanes] = own.astype(jnp.bfloat16)


def whiten(lengths, own_mask, near_mask, own, near, tables, touched):
    smem = pl.BlockSpec(memory_space=pltpu.SMEM)
    vmem = pl.BlockSpec(memory_space=pltpu.VMEM)
    return pl.pallas_call(
        whiten_kernel,
        in_specs=[smem, smem, smem, vmem, vmem, vmem, vmem, vmem],
        out_specs=[vmem, vmem],
        out_shape=[jax.ShapeDtypeStruct((rows, 4 * F), jnp.bfloat16) for rows in (16, 8)],
        compiler_params=pltpu.CompilerParams(vmem_limit_bytes=16 * 2**20),
        name="whiten",
    )(lengths, own_mask, near_mask, own, near, *tables, touched)


def fold_kernel(own_ref, other_ref, lag_ref, out_ref, rows):
    i = pl.program_id(0)
    rows[0] = own_ref[...].astype(jnp.float32)
    rows[1] = other_ref[...].astype(jnp.float32)
    mine = 4 * lax.axis_index("tm") + i
    step = 32

    @pl.loop(0, 2 * LAG, step=step)
    def _(begin):
        at = pl.ds(pl.multiple_of(begin, step), step)
        cos = lag_ref[at, :F].astype(jnp.float32)
        sin = lag_ref[at, F:].astype(jnp.float32)
        for group in range(2):
            for k in range(2):
                to = 2 * F * (2 * group + k)
                a_re = rows[group, pl.ds(mine, 1), 2 * k * F : (2 * k + 1) * F]
                a_im = rows[group, pl.ds(mine, 1), (2 * k + 1) * F : (2 * k + 2) * F]
                out_ref[at, to : to + F] = (a_re * cos + a_im * sin).astype(jnp.bfloat16)
                out_ref[at, to + F : to + 2 * F] = (a_im * cos - a_re * sin).astype(jnp.bfloat16)


def fold(own, other):
    whole = pl.BlockSpec((8, 4 * F), lambda i: (0, 0))
    return pl.pallas_call(
        fold_kernel,
        grid=(4,),
        in_specs=[whole, whole, pl.BlockSpec((2 * LAG, 2 * F), lambda i: (0, 0))],
        out_specs=pl.BlockSpec((2 * LAG, 8 * F), lambda i: (i, 0)),
        out_shape=jax.ShapeDtypeStruct((8 * LAG, 8 * F), jnp.bfloat16),
        scratch_shapes=[pltpu.VMEM((2, 8, 4 * F), jnp.float32)],
        cost_estimate=pl.CostEstimate(flops=2**20, bytes_accessed=2**10, transcendentals=0),
        compiler_params=pltpu.CompilerParams(vmem_limit_bytes=16 * 2**20),
        name="fold",
    )(own, other, jnp.asarray(np.ascontiguousarray(lag_table().T)))


ALL, TOP, BOTTOM = slice(0, 256), slice(0, 128), slice(128, 256)
NEAR = {
    0: ([(0, TOP), (1, TOP)], [(2, TOP), (3, TOP)], [(b, 1) for b in range(4)]),
    1: ([(0, TOP), (2, TOP)], [(1, TOP), (3, TOP)], [(1, 0), (1, 1), (3, 0), (3, 1)]),
}
FAR = {
    0: (None, [(2, TOP), (3, TOP)], [(b, 0) for b in range(4)]),
    1: ([(0, TOP), (2, TOP)], [(1, TOP), (3, TOP)], [(0, 0), (0, 1), (2, 0), (2, 1)]),
}


NEAR_TOO = {
    0: ([(0, TOP), (1, TOP)], [(0, BOTTOM), (1, BOTTOM)], NEAR[0][2]),
    1: ([(0, ALL)], [(1, ALL)], NEAR[1][2]),
}
FAR_TOO = {
    0: (None, [(1, TOP), (2, TOP)], FAR[0][2]),
    1: ([(0, TOP), (1, TOP)], [(0, BOTTOM), (2, TOP)], FAR[1][2]),
}


def part_kernel(work, earlier, has_early, last, count, *refs):
    refs = list(refs)
    chunks, folded = [refs.pop(0) for _ in range(count)], refs.pop(0)
    early = refs.pop(0) if has_early else None
    before = refs.pop(0) if earlier else None
    out_ref = refs.pop(0) if earlier else None
    result, sent = refs
    y, z, xl, core = (lax.axis_index(name) for name in ("y", "z", "xl", "core"))
    half = 4 * F

    def product(mine, pieces, columns):
        rows = [mine[p][at, :] for p, at in pieces]
        rows = rows[0] if len(rows) == 1 else jnp.concatenate(rows, axis=0)
        return lax.dot_general(rows, columns, (((1,), (1,)), ((), ())), preferred_element_type=jnp.float32)

    def copies_of(source, kind, offsets, i, slot):
        return [
            pltpu.make_async_copy(source.at[i, n], out_ref.at[i, y ^ dy, :, xl ^ dxl, kind], sent.at[slot, i, n])
            for n, (dy, dxl) in enumerate(offsets)
        ]

    def run(c):
        copies = []
        if earlier:
            for i in range(4):
                copies += copies_of(before, earlier[c][0], earlier[c][1][2], i, 0)
        for copy in copies:
            copy.start()
        kind, (first, second, offsets) = work[c]
        for i in range(4):
            at = slice(2 * LAG * i, 2 * LAG * (i + 1))
            values = early[:, at] if first is None else product(chunks, first, folded[at, :half])
            values += product(chunks, second, folded[at, half:])
            for n in range(len(offsets)):
                for g in range(NZ):
                    result[i, n, z ^ Z_ORDER[g]] = values[64 * n + 8 * g : 64 * n + 8 * g + 8]
            if last:
                own = copies_of(result, kind, offsets, i, 1)
                for copy in own:
                    copy.start()
                copies += own
        for copy in copies:
            copy.wait()

    for c in range(2):

        @pl.when(core == c)
        def _():
            run(c)


RESULT = (4, 4, NZ, 8, 2 * LAG)
VMEM_SPEC = pl.BlockSpec(memory_space=pltpu.VMEM)
HBM_SPEC = pl.BlockSpec(memory_space=pltpu.HBM)
OUT = jax.ShapeDtypeStruct((4, NY, NZ, 2, 2, 8, 2 * LAG), jnp.float32)
SMALL = pl.CostEstimate(flops=2**20, bytes_accessed=2**10, transcendentals=0)


def correlate_part(work, chunks, folded, early=None, before=None, earlier=None, out=None, last=False):
    operands = [*chunks, folded] + [array for array in (early, before) if array is not None]
    in_specs = [VMEM_SPEC] * len(operands)
    aliases = {}
    if out is not None:
        aliases = {len(operands): 0}
        operands, in_specs = [*operands, out], [*in_specs, HBM_SPEC]
    results = ([(HBM_SPEC, OUT)] if earlier else []) + (
        [] if last else [(VMEM_SPEC, jax.ShapeDtypeStruct(RESULT, jnp.float32))]
    )
    kernel = functools.partial(part_kernel, work, earlier, early is not None, last, len(chunks))
    return pl.pallas_call(
        kernel if out is None else lambda *refs: kernel(*refs[: len(operands) - 1], *refs[len(operands) :]),
        in_specs=in_specs,
        out_specs=[spec for spec, _ in results],
        out_shape=[shape for _, shape in results],
        scratch_shapes=([pltpu.VMEM(RESULT, jnp.float32)] if last else []) + [pltpu.SemaphoreType.DMA((2, 4, 4))],
        input_output_aliases=aliases,
        cost_estimate=SMALL,
        compiler_params=pltpu.CompilerParams(vmem_limit_bytes=24 * 2**20),
        name="correlate",
    )(*operands)


def plane_kernel(earlier, top, bottom, plane_too, folded, before, _, out_ref, early, sent):
    y, xl, core = (lax.axis_index(name) for name in ("y", "xl", "core"))

    def run(c, rows):
        kind, (_, _, offsets) = earlier[c]
        copies = [
            pltpu.make_async_copy(before.at[i, n], out_ref.at[i, y ^ dy, :, xl ^ dxl, kind], sent.at[i, n])
            for i in range(4)
            for n, (dy, dxl) in enumerate(offsets)
        ]
        for copy in copies:
            copy.start()
        early[...] = lax.dot_general(
            jnp.concatenate([half[...] for half in rows], axis=0),
            folded[:, : 4 * F],
            (((1,), (1,)), ((), ())),
            preferred_element_type=jnp.float32,
        )
        for copy in copies:
            copy.wait()

    for c in range(2):

        @pl.when(core == c)
        def _():
            run(c, ((top, bottom), (plane_too,))[c])


def correlate_plane(mine, theirs, folded, before, earlier, out):
    return pl.pallas_call(
        functools.partial(plane_kernel, earlier),
        in_specs=[VMEM_SPEC] * 5 + [HBM_SPEC],
        out_specs=[HBM_SPEC, VMEM_SPEC],
        out_shape=[OUT, jax.ShapeDtypeStruct((256, 8 * LAG), jnp.float32)],
        scratch_shapes=[pltpu.SemaphoreType.DMA((4, 4))],
        input_output_aliases={5: 0},
        cost_estimate=SMALL,
        compiler_params=pltpu.CompilerParams(vmem_limit_bytes=24 * 2**20),
        name="plane",
    )(*mine, theirs, folded, before, out)


def of_own_class(part):
    return [(kind, part[kind]) for kind in (0, 1)]


def of_other_class(part):
    return [(kind, part[kind]) for kind in (1, 0)]


def local(traces, lengths, mask):
    near_traces, near_mask = permute(traces, along_z(2)), permute(mask, along_z(2))
    tables = [jnp.asarray(table) for table in dft_tables()]
    near_traces, near_mask, touched = lax.optimization_barrier((near_traces, near_mask, touch(tables)))
    pair, own = whiten(lengths, mask, near_mask, traces, near_traces, tables, touched)
    ring = jnp.concatenate([pair] + [permute(pair, along_z(d)) for d in (1, 6, 7)], axis=0)
    other = permute(own, other_group)
    ring, own, other = lax.optimization_barrier((ring, own, other))
    first = [permute(ring, along_first(d)) for d in range(1, 4)]
    top = jnp.concatenate([ring, first[0]], axis=0)
    bottom = jnp.concatenate(first[1:], axis=0)
    near_bottom = [permute(bottom, along_second(d)) for d in (1, 3)]
    near_top = [permute(top, along_second(d)) for d in (1, 3)]
    folded = fold(own, other)
    near = [near_top[0], near_bottom[0], near_top[1], near_bottom[1]]
    tops = jnp.concatenate([near_top[0], near_top[1]], axis=0)
    plane = jnp.concatenate([top, bottom], axis=0)
    *near, top, bottom, folded, tops, plane = lax.optimization_barrier((*near, top, bottom, folded, tops, plane))
    far = [permute(near[2], along_second(1)), permute(near[1], along_second(3))]
    bottoms = jnp.concatenate([near[1], near[3]], axis=0)
    near_too = [permute(chunk, other_core) for chunk in (tops, bottoms)]
    plane_too = permute(plane, other_core)
    (before,) = correlate_part(of_own_class(NEAR), near, folded)
    out, before = correlate_part(of_other_class(NEAR_TOO), near_too, folded, before=before, earlier=of_own_class(NEAR))
    plane_too, before, out = lax.optimization_barrier((plane_too, before, out))
    out, early = correlate_plane([top, bottom], plane_too, folded, before, of_other_class(NEAR), out)
    far[0], far[1], out, early = lax.optimization_barrier((*far, out, early))
    far_too = [permute(half, other_core) for half in far]
    (before,) = correlate_part(of_own_class(FAR), [top, bottom, *far], folded, early)
    (out,) = correlate_part(
        of_other_class(FAR_TOO),
        [plane_too, *far_too],
        folded,
        early,
        before=before,
        earlier=of_own_class(FAR),
        out=out,
        last=True,
    )
    return out.reshape(4, NY * NZ * 4 * 8, 2 * LAG)


def solution(mesh):
    finer = Mesh(mesh.devices.reshape(NY, NZ, 2, 2, 2), AXES)
    chan = ("y", "z", "xl", "core")
    return jax.shard_map(
        local,
        mesh=finer,
        in_specs=(P("tm", chan, None), P(), P(chan)),
        out_specs=P(AXES, None, None),
        check_vma=False,
    )
```

```python
import functools
import math

import jax
import jax.numpy as jnp
import ml_dtypes
import numpy as np
from jax import lax
from jax.experimental import pallas as pl
from jax.experimental.pallas import tpu as pltpu
from jax.sharding import Mesh
from jax.sharding import PartitionSpec as P

NFFT = 1024
LAG = 128
F = 512
SEG = 768
SUBWIN = 4
NY, NZ, NX = 4, 8, 4
Z_ORDER = (0, 2, 1, 3, 6, 4, 7, 5)
AXES = ("y", "z", "xl", "core", "tm")


def dft_tables():
    product = np.mod(np.arange(SEG)[:, None] * np.arange(F)[None, :], NFFT)
    theta = product * (2.0 * math.pi / NFFT)
    table = np.concatenate([np.cos(theta), -np.sin(theta)], axis=1)
    high = table.astype(ml_dtypes.bfloat16)
    low = (table - high.astype(np.float64)).astype(ml_dtypes.bfloat16)
    return high, low


def lag_table():
    product = np.mod(np.arange(F)[:, None] * (np.arange(2 * LAG) - LAG)[None, :], NFFT)
    phase = product * (2.0 * math.pi / NFFT)
    weight = np.where(np.arange(F) == 0, 1.0, 2.0)[:, None] / math.sqrt(F * SUBWIN)
    table = np.concatenate([weight * np.cos(phase), -weight * np.sin(phase)], axis=0)
    return table.astype(np.float32).astype(ml_dtypes.bfloat16)


def device_index(y, z, x, core):
    return (((y * NZ + z) * 2 + x % 2) * 2 + core) * 2 + x // 2


def permute(value, partner):
    pairs = []
    for y in range(NY):
        for z in range(NZ):
            for x in range(NX):
                for core in range(2):
                    pairs.append((device_index(y, z, x, core), device_index(*partner(y, z, x, core))))
    return lax.ppermute(value, AXES, pairs)


def along_z(d):
    return lambda y, z, x, core: (y, z ^ d, x, core)


def along_first(d):
    return lambda y, z, x, core: (y ^ d, z, x, core) if core == 0 else (y, z, x ^ d, core)


def along_second(d):
    return lambda y, z, x, core: (y, z, x ^ d, core) if core == 0 else (y ^ d, z, x, core)


def other_core(y, z, x, core):
    return (y, z, x, 1 - core)


def other_group(y, z, x, core):
    return (y, z, x ^ 2, core)


def touch_kernel(high_ref, low_ref, out_ref):
    out_ref[...] = high_ref[0:16, 0:128] + low_ref[0:16, 0:128]


def touch(tables):
    vmem = pl.BlockSpec(memory_space=pltpu.VMEM)
    return pl.pallas_call(
        touch_kernel,
        in_specs=[vmem, vmem],
        out_specs=vmem,
        out_shape=jax.ShapeDtypeStruct((16, 128), jnp.bfloat16),
        cost_estimate=pl.CostEstimate(flops=2**10, bytes_accessed=2**10, transcendentals=0),
        compiler_params=pltpu.CompilerParams(vmem_limit_bytes=16 * 2**20),
        name="touch",
    )(*tables)


def whiten_kernel(lengths_ref, own_mask_ref, near_mask_ref, own_ref, near_ref, high_ref, low_ref, touched_ref, pair_ref, out_ref):
    del touched_ref
    tm = lax.axis_index("tm")
    x = jnp.concatenate([own_ref[...].reshape(16, SEG), near_ref[...].reshape(16, SEG)], axis=0)
    row = lax.broadcasted_iota(jnp.int32, (32, 1), 0)
    length = jnp.where(row % 16 < 8, lengths_ref[2 * tm], lengths_ref[2 * tm + 1])
    usable = jnp.zeros((32, 1), jnp.float32)
    for c in range(8):
        mask = jnp.where(row < 16, own_mask_ref[c], near_mask_ref[c])
        usable = jnp.where(row % 8 == c, mask.astype(jnp.float32), usable)
    live = lax.broadcasted_iota(jnp.int32, (32, SEG), 1) < length
    average = jnp.sum(jnp.where(live, x, 0.0), axis=1, keepdims=True) / length.astype(jnp.float32)
    centred = jnp.where(live, x - average, 0.0)
    part0 = centred.astype(jnp.bfloat16)
    rest = centred - part0.astype(jnp.float32)
    part1 = rest.astype(jnp.bfloat16)
    part2 = (rest - part1.astype(jnp.float32)).astype(jnp.bfloat16)
    parts = jnp.concatenate([part0, part1, part2], axis=0)
    by_high = jnp.dot(parts, high_ref[...], preferred_element_type=jnp.float32)
    by_low = jnp.dot(parts[:64], low_ref[...], preferred_element_type=jnp.float32)
    spectrum = by_high[:32] + (by_high[32:64] + by_low[:32] + (by_high[64:] + by_low[32:]))
    re, im = spectrum[:, :F], spectrum[:, F:]
    power = re * re + im * im
    level = jnp.mean(power, axis=1, keepdims=True)
    factor = usable / jnp.sqrt(power + 0.01 * level + 1e-06)
    white = [re * factor, im * factor]
    for k in range(2):
        for part in range(2):
            lanes = slice((2 * k + part) * F, (2 * k + part + 1) * F)
            own = white[part][8 * k : 8 * k + 8]
            pair_ref[:, lanes] = jnp.concatenate([own, white[part][16 + 8 * k : 24 + 8 * k]], axis=0).astype(jnp.bfloat16)
            out_ref[:, lanes] = own.astype(jnp.bfloat16)


def whiten(lengths, own_mask, near_mask, own, near, tables, touched):
    smem = pl.BlockSpec(memory_space=pltpu.SMEM)
    vmem = pl.BlockSpec(memory_space=pltpu.VMEM)
    return pl.pallas_call(
        whiten_kernel,
        in_specs=[smem, smem, smem, vmem, vmem, vmem, vmem, vmem],
        out_specs=[vmem, vmem],
        out_shape=[jax.ShapeDtypeStruct((rows, 4 * F), jnp.bfloat16) for rows in (16, 8)],
        compiler_params=pltpu.CompilerParams(vmem_limit_bytes=16 * 2**20),
        name="whiten",
    )(lengths, own_mask, near_mask, own, near, *tables, touched)


def fold_kernel(own_ref, other_ref, lag_ref, out_ref, rows):
    i = pl.program_id(0)
    rows[0] = own_ref[...].astype(jnp.float32)
    rows[1] = other_ref[...].astype(jnp.float32)
    mine = 4 * lax.axis_index("tm") + i
    step = 32

    @pl.loop(0, 2 * LAG, step=step)
    def _(begin):
        at = pl.ds(pl.multiple_of(begin, step), step)
        cos = lag_ref[at, :F].astype(jnp.float32)
        sin = lag_ref[at, F:].astype(jnp.float32)
        for group in range(2):
            for k in range(2):
                to = 2 * F * (2 * group + k)
                a_re = rows[group, pl.ds(mine, 1), 2 * k * F : (2 * k + 1) * F]
                a_im = rows[group, pl.ds(mine, 1), (2 * k + 1) * F : (2 * k + 2) * F]
                out_ref[at, to : to + F] = (a_re * cos + a_im * sin).astype(jnp.bfloat16)
                out_ref[at, to + F : to + 2 * F] = (a_im * cos - a_re * sin).astype(jnp.bfloat16)


def fold(own, other):
    whole = pl.BlockSpec((8, 4 * F), lambda i: (0, 0))
    return pl.pallas_call(
        fold_kernel,
        grid=(4,),
        in_specs=[whole, whole, pl.BlockSpec((2 * LAG, 2 * F), lambda i: (0, 0))],
        out_specs=pl.BlockSpec((2 * LAG, 8 * F), lambda i: (i, 0)),
        out_shape=jax.ShapeDtypeStruct((8 * LAG, 8 * F), jnp.bfloat16),
        scratch_shapes=[pltpu.VMEM((2, 8, 4 * F), jnp.float32)],
        cost_estimate=pl.CostEstimate(flops=2**20, bytes_accessed=2**10, transcendentals=0),
        compiler_params=pltpu.CompilerParams(vmem_limit_bytes=16 * 2**20),
        name="fold",
    )(own, other, jnp.asarray(np.ascontiguousarray(lag_table().T)))


ALL, TOP, BOTTOM = slice(0, 256), slice(0, 128), slice(128, 256)
NEAR = {
    0: ([(0, TOP), (1, TOP)], [(2, TOP), (3, TOP)], [(b, 1) for b in range(4)]),
    1: ([(0, TOP), (2, TOP)], [(1, TOP), (3, TOP)], [(1, 0), (1, 1), (3, 0), (3, 1)]),
}
FAR = {
    0: (None, [(2, TOP), (3, TOP)], [(b, 0) for b in range(4)]),
    1: ([(0, TOP), (2, TOP)], [(1, TOP), (3, TOP)], [(0, 0), (0, 1), (2, 0), (2, 1)]),
}


NEAR_TOO = {
    0: ([(0, TOP), (1, TOP)], [(0, BOTTOM), (1, BOTTOM)], NEAR[0][2]),
    1: ([(0, ALL)], [(1, ALL)], NEAR[1][2]),
}
FAR_TOO = {
    0: (None, [(1, TOP), (2, TOP)], FAR[0][2]),
    1: ([(0, TOP), (1, TOP)], [(0, BOTTOM), (2, TOP)], FAR[1][2]),
}


def part_kernel(work, earlier, has_early, last, count, *refs):
    refs = list(refs)
    chunks, folded = [refs.pop(0) for _ in range(count)], refs.pop(0)
    early = refs.pop(0) if has_early else None
    before = refs.pop(0) if earlier else None
    out_ref = refs.pop(0) if earlier else None
    result, sent = refs
    y, z, xl, core = (lax.axis_index(name) for name in ("y", "z", "xl", "core"))
    half = 4 * F

    def product(mine, pieces, columns):
        rows = [mine[p][at, :] for p, at in pieces]
        rows = rows[0] if len(rows) == 1 else jnp.concatenate(rows, axis=0)
        return lax.dot_general(rows, columns, (((1,), (1,)), ((), ())), preferred_element_type=jnp.float32)

    def copies_of(source, kind, offsets, i, slot):
        return [
            pltpu.make_async_copy(source.at[i, n], out_ref.at[i, y ^ dy, :, xl ^ dxl, kind], sent.at[slot, i, n])
            for n, (dy, dxl) in enumerate(offsets)
        ]

    def run(c):
        copies = []
        if earlier:
            for i in range(4):
                copies += copies_of(before, earlier[c][0], earlier[c][1][2], i, 0)
        for copy in copies:
            copy.start()
        kind, (first, second, offsets) = work[c]
        for i in range(4):
            at = slice(2 * LAG * i, 2 * LAG * (i + 1))
            values = early[:, at] if first is None else product(chunks, first, folded[at, :half])
            values += product(chunks, second, folded[at, half:])
            own = copies_of(result, kind, offsets, i, 1) if last else []
            for n in range(len(offsets)):
                for g in range(NZ):
                    result[i, n, z ^ Z_ORDER[g]] = values[64 * n + 8 * g : 64 * n + 8 * g + 8]
                if last:
                    own[n].start()
            copies += own
        for copy in copies:
            copy.wait()

    for c in range(2):

        @pl.when(core == c)
        def _():
            run(c)


RESULT = (4, 4, NZ, 8, 2 * LAG)
VMEM_SPEC = pl.BlockSpec(memory_space=pltpu.VMEM)
HBM_SPEC = pl.BlockSpec(memory_space=pltpu.HBM)
OUT = jax.ShapeDtypeStruct((4, NY, NZ, 2, 2, 8, 2 * LAG), jnp.float32)
SMALL = pl.CostEstimate(flops=2**20, bytes_accessed=2**10, transcendentals=0)


def correlate_part(work, chunks, folded, early=None, before=None, earlier=None, out=None, last=False):
    operands = [*chunks, folded] + [array for array in (early, before) if array is not None]
    in_specs = [VMEM_SPEC] * len(operands)
    aliases = {}
    if out is not None:
        aliases = {len(operands): 0}
        operands, in_specs = [*operands, out], [*in_specs, HBM_SPEC]
    results = ([(HBM_SPEC, OUT)] if earlier else []) + (
        [] if last else [(VMEM_SPEC, jax.ShapeDtypeStruct(RESULT, jnp.float32))]
    )
    kernel = functools.partial(part_kernel, work, earlier, early is not None, last, len(chunks))
    return pl.pallas_call(
        kernel if out is None else lambda *refs: kernel(*refs[: len(operands) - 1], *refs[len(operands) :]),
        in_specs=in_specs,
        out_specs=[spec for spec, _ in results],
        out_shape=[shape for _, shape in results],
        scratch_shapes=([pltpu.VMEM(RESULT, jnp.float32)] if last else []) + [pltpu.SemaphoreType.DMA((2, 4, 4))],
        input_output_aliases=aliases,
        cost_estimate=SMALL,
        compiler_params=pltpu.CompilerParams(vmem_limit_bytes=24 * 2**20),
        name="correlate",
    )(*operands)


def plane_kernel(earlier, top, bottom, plane_too, folded, before, _, out_ref, early, sent):
    y, xl, core = (lax.axis_index(name) for name in ("y", "xl", "core"))

    def run(c, rows):
        kind, (_, _, offsets) = earlier[c]
        copies = [
            pltpu.make_async_copy(before.at[i, n], out_ref.at[i, y ^ dy, :, xl ^ dxl, kind], sent.at[i, n])
            for i in range(4)
            for n, (dy, dxl) in enumerate(offsets)
        ]
        for copy in copies:
            copy.start()
        early[...] = lax.dot_general(
            jnp.concatenate([half[...] for half in rows], axis=0),
            folded[:, : 4 * F],
            (((1,), (1,)), ((), ())),
            preferred_element_type=jnp.float32,
        )
        for copy in copies:
            copy.wait()

    for c in range(2):

        @pl.when(core == c)
        def _():
            run(c, ((top, bottom), (plane_too,))[c])


def correlate_plane(mine, theirs, folded, before, earlier, out):
    return pl.pallas_call(
        functools.partial(plane_kernel, earlier),
        in_specs=[VMEM_SPEC] * 5 + [HBM_SPEC],
        out_specs=[HBM_SPEC, VMEM_SPEC],
        out_shape=[OUT, jax.ShapeDtypeStruct((256, 8 * LAG), jnp.float32)],
        scratch_shapes=[pltpu.SemaphoreType.DMA((4, 4))],
        input_output_aliases={5: 0},
        cost_estimate=SMALL,
        compiler_params=pltpu.CompilerParams(vmem_limit_bytes=24 * 2**20),
        name="plane",
    )(*mine, theirs, folded, before, out)


def of_own_class(part):
    return [(kind, part[kind]) for kind in (0, 1)]


def of_other_class(part):
    return [(kind, part[kind]) for kind in (1, 0)]


def local(traces, lengths, mask):
    near_traces, near_mask = permute(traces, along_z(2)), permute(mask, along_z(2))
    tables = [jnp.asarray(table) for table in dft_tables()]
    near_traces, near_mask, touched = lax.optimization_barrier((near_traces, near_mask, touch(tables)))
    pair, own = whiten(lengths, mask, near_mask, traces, near_traces, tables, touched)
    ring = jnp.concatenate([pair] + [permute(pair, along_z(d)) for d in (1, 6, 7)], axis=0)
    other = permute(own, other_group)
    ring, own, other = lax.optimization_barrier((ring, own, other))
    first = [permute(ring, along_first(d)) for d in range(1, 4)]
    top = jnp.concatenate([ring, first[0]], axis=0)
    bottom = jnp.concatenate(first[1:], axis=0)
    near_bottom = [permute(bottom, along_second(d)) for d in (1, 3)]
    near_top = [permute(top, along_second(d)) for d in (1, 3)]
    folded = fold(own, other)
    near = [near_top[0], near_bottom[0], near_top[1], near_bottom[1]]
    tops = jnp.concatenate([near_top[0], near_top[1]], axis=0)
    plane = jnp.concatenate([top, bottom], axis=0)
    *near, top, bottom, folded, tops, plane = lax.optimization_barrier((*near, top, bottom, folded, tops, plane))
    far = [permute(near[2], along_second(1)), permute(near[1], along_second(3))]
    bottoms = jnp.concatenate([near[1], near[3]], axis=0)
    near_too = [permute(chunk, other_core) for chunk in (tops, bottoms)]
    plane_too = permute(plane, other_core)
    (before,) = correlate_part(of_own_class(NEAR), near, folded)
    out, before = correlate_part(of_other_class(NEAR_TOO), near_too, folded, before=before, earlier=of_own_class(NEAR))
    plane_too, before, out = lax.optimization_barrier((plane_too, before, out))
    out, early = correlate_plane([top, bottom], plane_too, folded, before, of_other_class(NEAR), out)
    far[0], far[1], out, early = lax.optimization_barrier((*far, out, early))
    far_too = [permute(half, other_core) for half in far]
    (before,) = correlate_part(of_own_class(FAR), [top, bottom, *far], folded, early)
    (out,) = correlate_part(
        of_other_class(FAR_TOO),
        [plane_too, *far_too],
        folded,
        early,
        before=before,
        earlier=of_own_class(FAR),
        out=out,
        last=True,
    )
    return out.reshape(4, NY * NZ * 4 * 8, 2 * LAG)


def solution(mesh):
    finer = Mesh(mesh.devices.reshape(NY, NZ, 2, 2, 2), AXES)
    chan = ("y", "z", "xl", "core")
    return jax.shard_map(
        local,
        mesh=finer,
        in_specs=(P("tm", chan, None), P(), P(chan)),
        out_specs=P(AXES, None, None),
        check_vma=False,
    )
```
